128 devices in a mesh: tgt: 2 (over z_hi), fsdp: 16 (over z_lo, x, core), dp: 4 (over y).
Axes of the slice: x: 4, y: 4, z: 4 (z_hi: 2, z_lo: 2; z = z_hi * 2 + z_lo), core: 2. Of those that a mesh axis runs over, the one named last changes fastest.
Arguments:
- tokens: bfloat16 [49152, 1408], P(('tgt', 'fsdp', 'dp')), may hold values from -6 to 6
- widen_weight: bfloat16 [1408, 6144], P(None, 'fsdp'), may hold values from -0.15625 to 0.15625
- narrow_weight: bfloat16 [6144, 1408], P(None, 'fsdp'), may hold values from -0.078125 to 0.078125
- head_weight: bfloat16 [384, 1408], P(None, 'fsdp'), may hold values from -0.3125 to 0.3125
- predictor_rows: bfloat16 [131072, 384], P(('tgt', 'fsdp', 'dp')), may hold values from -24 to 24
- target_index: int32 [32768], P(('tgt', 'fsdp', 'dp')), may hold values from 0 to 383, as said below
- destination: int32 [32768, 1], P(('tgt', 'fsdp', 'dp')), may hold values from 0 to 31; in each aligned block of 256 rows (0 to 255, 256 to 511, ...) at most 32 rows name the same one
Outputs:
- target_features: bfloat16 [49152, 1408], P(('tgt', 'fsdp', 'dp'))
- target_error: bfloat16 [131072, 1408], P(('tgt', 'fsdp', 'dp'))
- head_gradient: float32 [384, 1408], P('fsdp')
The draws below stay inside these ranges and needn't reach their ends.
Inputs may be any that keep to these rules, and one draw needn't show every extreme that they name: `target_index`: each block of 256 entries lists distinct rows of its device, in rising order. `destination`: among the 256 rows of one device no owner is named more than 32 times, a bound that some block reaches.
All inputs are finite; a program needn't handle non-finite values.
Results may differ from the reference program's by a relative error of at most 0.015.
Values may be sent and summed in bfloat16 or wider, within the bound.
A program may use at most 128 MiB of HBM per device.

```python
import math
import jax
import jax.numpy as jnp
import numpy as np
from jax import lax

D = 1408
FF = 6144
P_SIZE = 384
TOK_DEV = 384
SEL = 256
CAP = 32
NDEST = 32
TOKENS = 49152
SLOTS = 131072
N_TGT = 2
N_FSDP = 16
N_DP = 4


def draw_target_index(key, part):
    key = jax.random.fold_in(key, 11)
    subkeys = jax.random.split(key, N_TGT * N_FSDP * N_DP)

    def choose(subkey):
        shuffled = jax.random.permutation(subkey, TOK_DEV)
        return jnp.sort(shuffled[:SEL]).astype(jnp.int32)
    return jax.vmap(choose)(subkeys).reshape(-1)


def with_spikes(entries, key, source, target, blocks, factor):
    owner, partner = [(jnp.arange(entries.shape[dim]) // (entries.shape[dim] // blocks)).reshape([-1 if axis == dim else 1 for axis in range(entries.ndim)]) for dim in (source, target)]
    chosen = jax.random.permutation(key, blocks)[partner]
    strong = (owner == chosen) | (owner == (partner + blocks // 2) % blocks)
    return jnp.where(strong, factor * entries, entries)


def shard_levels(key, shape, shards, smallest, high):
    def one(axis_at, blocks):
        draws = jax.random.uniform(jax.random.fold_in(jax.random.fold_in(key, 6), axis_at), (blocks,), jnp.float32, smallest / len(shards), high / len(shards))
        return jnp.repeat(jnp.exp(draws), shape[axis_at] // blocks).reshape((-1,) + (1,) * (len(shape) - axis_at - 1))

    factor_of = one(*shards[0])
    for cut in shards[1:]:
        factor_of = factor_of * one(*cut)
    return factor_of


def assign_block(own_key, own, number, rows, count, top, bound, slope):
    ranking = jax.random.permutation(own_key, count)
    heavy_load, ordinary = shares(count, rows * top, bound, slope, True), shares(count, rows * top, bound, slope, False)
    places = jnp.arange(count)

    def named(lengths, rotation):
        used = int((lengths > 0).sum())
        fixed = max(1, used // 4)
        moved = fixed + (places - fixed + rotation * (used - fixed)) % max(1, count - fixed)
        return jnp.zeros((count,), jnp.int32).at[ranking[jnp.where(places < fixed, places, moved)]].set(jnp.asarray(lengths, jnp.int32))

    lengths = jnp.where(number % 4 == 0, named(heavy_load, number // 4), named(ordinary, number - number // 4 - 1))
    mixed = jax.random.permutation(jax.random.fold_in(own, 3), count)
    donor, receiver = mixed[0:count // 2 * 2:2], mixed[1:count // 2 * 2:2]
    slack = jnp.minimum(lengths[donor] - 1, bound - lengths[receiver]) // 2
    slack = jnp.where((donor == ranking[0]) | (receiver == ranking[0]) | (lengths[receiver] == 0), 0, jnp.maximum(slack, 0))
    moved = jax.random.randint(jax.random.fold_in(own, 4), (count // 2,), 0, 1 << 20) % (slack + 1)
    lengths = lengths.at[donor].add(-moved).at[receiver].add(moved)
    labels = jnp.searchsorted(jnp.cumsum(lengths), jnp.arange(rows * top), side="right").astype(jnp.int32)
    table = labels.reshape(top, rows).T
    table = table[jax.random.permutation(jax.random.fold_in(own, 1), rows)]
    rotation = jax.random.randint(jax.random.fold_in(own, 2), (rows, 1), 0, top)
    return jnp.take_along_axis(table, (jnp.arange(top)[None, :] + rotation) % top, axis=1)


def shares(number_of, total, bound, slope, full):
    portions = [(1 << 20) // math.isqrt(rank ** slope) + 1 for rank in range(1, number_of + 1)]
    largest = bound if full else min(bound, max(-(-total // number_of), total * portions[0] // sum(portions)))
    least = 1 if total - largest >= number_of - 1 else 0
    counts, rest = [largest] + [least] * (number_of - 1), total - largest - least * (number_of - 1)
    while rest > 0:
        movable = [i for i in range(1, number_of) if counts[i] < largest] or [i for i in range(1, number_of) if counts[i] < bound]
        mass, budget = sum([portions[i] for i in movable]), rest
        for i in movable:
            addition = min(bound - counts[i], max(1, budget * portions[i] // mass), rest)
            counts[i] = counts[i] + addition
            rest = rest - addition
    return np.array(counts)


def centred(own_key, dims, scale, most, cuts=(), held_as=jnp.bfloat16):
    entries = jax.random.normal(own_key, dims, jnp.float32) * scale
    if len(cuts) > 0:
        entries = shard_levels(own_key, dims, cuts, -0.22, 0.18) * entries
    return jnp.clip(entries, min=-most, max=most).astype(held_as)


def noise_with(own_key, dims, width, reach, cuts, heavy, kind=jnp.bfloat16):
    values = width * jax.random.normal(own_key, dims, jnp.float32)
    if cuts:
        values = values * shard_levels(own_key, dims, cuts, -0.22, 0.18)
    return jnp.clip(with_spikes(values, jax.random.fold_in(own_key, 3), *heavy), -reach, reach).astype(kind)


def setup_inputs(seed: int = 0) -> dict:
    splits = jax.random.split(jax.random.key(seed), 8)
    tokens = centred(splits[0], (TOKENS, D), 1.0, 6.0, ((0, 128),))
    widen_weight = centred(splits[1], (D, FF), D ** -0.5, 0.15625, ((1, 16),))
    narrow_weight = centred(splits[2], (FF, D), FF ** -0.5, 0.078125, ((1, 16),))
    head_weight = centred(splits[3], (P_SIZE, D), P_SIZE ** -0.5, 0.3125, ((1, 16),))
    predictor_rows = noise_with(splits[4], (SLOTS, P_SIZE), 1.0, 24.0, ((0, 128),), (0, 1, 128, 5.5))
    target_index = draw_target_index(jax.random.fold_in(splits[7], 71), 0)
    destination_keys = jax.random.split(jax.random.fold_in(splits[6], 1), (N_TGT * N_FSDP * N_DP * SEL) // SEL)
    destination_turns = jax.random.permutation(jax.random.fold_in(splits[6], 3), (N_TGT * N_FSDP * N_DP * SEL) // SEL)
    destination = jax.vmap(lambda own, number: assign_block(jax.random.fold_in(splits[6], 2), own, number, SEL, NDEST, 1, CAP, 2))(destination_keys, destination_turns).reshape((N_TGT * N_FSDP * N_DP * SEL, 1))
    return {"tokens": tokens, "widen_weight": widen_weight, "narrow_weight": narrow_weight, "head_weight": head_weight, "predictor_rows": predictor_rows, "target_index": target_index, "destination": destination}


def norm_rows(values):
    center = lax.optimization_barrier(jnp.mean(values, axis=-1, keepdims=True))
    shifted = values - center
    spread = lax.optimization_barrier(jnp.mean(shifted * shifted, axis=-1, keepdims=True))
    return shifted * lax.rsqrt(spread + 1e-06)

def encode(block, widen_weight, narrow_weight):
    inputs = block.astype(jnp.float32)
    normed = norm_rows(inputs).astype(jnp.bfloat16)
    hidden = jax.nn.gelu(jnp.dot(normed, widen_weight, preferred_element_type=jnp.float32), approximate=False).astype(jnp.bfloat16)
    summed = inputs + jnp.dot(hidden, narrow_weight, preferred_element_type=jnp.float32)
    return norm_rows(summed).astype(jnp.bfloat16)

def reference(tokens, widen_weight, narrow_weight, head_weight, predictor_rows, target_index, destination):
    devices = N_TGT * N_FSDP * N_DP
    owners = N_TGT * N_FSDP
    blocks = tokens.reshape(devices, TOK_DEV, D)
    features = lax.map(lambda block: encode(block, widen_weight, narrow_weight), blocks)
    chosen = target_index.reshape(devices, SEL).astype(jnp.int32)
    picked = jnp.take_along_axis(features, chosen[:, :, None], axis=1)
    routed = destination.reshape(devices, SEL).astype(jnp.int32)
    onehot = (routed[:, :, None] == jnp.arange(owners, dtype=jnp.int32)[None, None, :]).astype(jnp.int32)
    before = jnp.cumsum(onehot, axis=1) - onehot
    slots = lax.optimization_barrier(jnp.sum(before * onehot, axis=2))
    source = jnp.arange(devices, dtype=jnp.int32)[:, None]
    owner_dev = routed * N_DP + source % N_DP
    position = ((owner_dev * owners + source // N_DP) * CAP + slots).reshape(-1).astype(jnp.int32)
    total_slots = devices * owners * CAP
    received = jnp.zeros((total_slots, D), jnp.bfloat16).at[position].set(picked.reshape(-1, D))
    filled = jnp.zeros((total_slots,), jnp.float32).at[position].set(1.0)
    prediction = jnp.dot(predictor_rows, head_weight, preferred_element_type=jnp.float32)
    mismatch = (filled[:, None] * (prediction - received.astype(jnp.float32))).astype(jnp.bfloat16)
    factor = 1.0 / math.sqrt(SEL * devices)
    gradient = jnp.dot(predictor_rows.T, mismatch, preferred_element_type=jnp.float32) * factor
    return (features.reshape(-1, D), mismatch, gradient)
```

```python
import functools
import math

import jax
import jax.numpy as jnp
from jax import lax
from jax.experimental import pallas as pl
from jax.experimental.pallas import tpu as pltpu
from jax.sharding import PartitionSpec as P

MESH = pl.DeviceIdType.MESH
F32, BF16 = jnp.float32, jnp.bfloat16


def norm_rows(values):
    center = jnp.mean(values, axis=-1, keepdims=True)
    shifted = values - center
    spread = jnp.mean(shifted * shifted, axis=-1, keepdims=True)
    return shifted * lax.rsqrt(spread + 1e-06)


def place():
    t, f, d = lax.axis_index("tgt"), lax.axis_index("fsdp"), lax.axis_index("dp")
    return lax.rem(f // 2, 4), d, 2 * t + f // 8, lax.rem(f, 2)


def device(x, y, z, c):
    return (z // 2, lax.rem(z, 2) * 8 + x * 2 + c, y)


def send(src, dst, send_sem, recv_sem, target):
    copy = pltpu.make_async_remote_copy(src, dst, send_sem, recv_sem, device_id=target, device_id_type=MESH)
    copy.start()


def wait_recv(dst, sem, target):
    pltpu.make_async_remote_copy(dst, dst, sem, sem, device_id=target, device_id_type=MESH).wait_recv()


def wait_send(src, sem, target):
    pltpu.make_async_remote_copy(src, src, sem, sem, device_id=target, device_id_type=MESH).wait_send()


def route_kernel(
    factor, cap, feat, tokpos, counts, rows, head, error, grad,
    buf, rcv, pred, flags, flags_in, gsum, gpad, pair_in, shares, r1, r2, fin, fin_in,
    s_a, r_a, s_f, r_f, s_0, r_0, s_1, r_1, s_2, r_2, s_3, r_3,
):
    x, y, z, c = place()
    t, zl = z // 2, lax.rem(z, 2)
    me = 8 * z + 2 * x + c
    owners = 32

    def plane(r):
        nx, nz, nc = lax.rem(x + lax.rem(r // 2, 4), 4), lax.rem(z + r // 8, 4), lax.rem(c + lax.rem(r, 2), 2)
        return device(nx, y, nz, nc), 8 * nz + 2 * nx + nc

    def plane_from(r):
        nx = lax.rem(x + 4 - lax.rem(r // 2, 4), 4)
        nz, nc = lax.rem(z + 4 - r // 8, 4), lax.rem(c + lax.rem(r, 2), 2)
        return device(nx, y, nz, nc), 8 * nz + 2 * nx + nc

    def group(j):
        nt, nd = lax.rem(t + j // 4, 2), lax.rem(y + lax.rem(j, 4), 4)
        return device(x, nd, 2 * nt + zl, c), nt * 4 + nd

    def chip(j):
        nz, nx = lax.rem(zl + j // 4, 2), lax.rem(x + lax.rem(j, 4), 4)
        return device(nx, y, 2 * t + nz, c), 4 * nz + nx

    partner = device(x, y, z, 1 - c)

    barrier = pltpu.get_barrier_semaphore()

    def greet(r, _):
        pl.semaphore_signal(barrier, inc=1, device_id=plane(r)[0], device_id_type=MESH)
        return 0

    lax.fori_loop(1, owners, greet, 0)

    def greet_group(j, _):
        @pl.when(lax.rem(j, 4) != 0)
        def _():
            pl.semaphore_signal(barrier, inc=1, device_id=group(j)[0], device_id_type=MESH)

        return 0

    lax.fori_loop(1, 8, greet_group, 0)

    slot_row = lax.broadcasted_iota(jnp.int32, (cap, 128), 0)
    flags[...] = jnp.where(slot_row < counts[...], 1.0, 0.0).astype(BF16)

    def fill(i, _):
        rows_at = pl.ds(pl.multiple_of(i * 128, 128), 128)
        slot = lax.broadcasted_iota(jnp.int32, (128, feat.shape[0]), 0) + i * 128
        pick = jnp.where(slot == tokpos[...], 1.0, 0.0).astype(BF16)
        buf[rows_at, :] = jnp.dot(pick, feat[...], preferred_element_type=F32).astype(BF16)
        return 0

    lax.fori_loop(0, owners * cap // 128, fill, 0)

    pl.semaphore_wait(barrier, owners - 1 + 6)

    def out(r, _):
        target, o = plane(r)
        send(flags, flags_in.at[me], s_f.at[o], r_f.at[me], target)
        src = buf.at[pl.ds(pl.multiple_of(o * cap, cap), cap)]
        send(src, rcv.at[pl.ds(pl.multiple_of(me * cap, cap), cap)], s_a.at[o], r_a.at[me], target)
        return 0

    lax.fori_loop(1, owners, out, 0)
    mine = pl.ds(pl.multiple_of(me * cap, cap), cap)
    rcv[mine, :] = buf[mine, :]
    flags_in[me] = flags[...]

    def predict(i, _):
        rows_at = pl.ds(pl.multiple_of(i * 128, 128), 128)
        pred[rows_at, :] = jnp.dot(rows[rows_at, :], head[...], preferred_element_type=F32)
        return 0

    lax.fori_loop(0, owners * cap // 128, predict, 0)
    gsum[...] = jnp.zeros_like(gsum)

    per = 8

    def arrive(k, _):
        i = lax.rem(z + k, 4)

        def one(q, _):
            s = i * per + q

            @pl.when(s != me)
            def _():
                wait_recv(flags_in.at[s], r_f.at[s], partner)
                wait_recv(rcv.at[pl.ds(pl.multiple_of(s * cap, cap), cap)], r_a.at[s], partner)

            return 0

        lax.fori_loop(0, per, one, 0)
        rows_at = pl.ds(pl.multiple_of(i * (per * cap), per * cap), per * cap)
        lane = lax.broadcasted_iota(jnp.int32, (per * cap, 128), 1)
        live = flags_in[pl.ds(i * per, per)].astype(F32).reshape(per * cap, 128)
        live = jnp.sum(jnp.where(lane == me, live, 0.0), axis=1, keepdims=True)
        wrong = jnp.where(live > 0.5, pred[rows_at, :] - rcv[rows_at, :].astype(F32), 0.0).astype(BF16)
        error[rows_at, :] = wrong
        gsum[...] += lax.dot_general(
            rows[rows_at, :], wrong, (((0,), (0,)), ((), ())), preferred_element_type=F32
        )
        return 0

    lax.fori_loop(0, 4, arrive, 0)

    wide = gsum.shape[1]
    half = gpad.shape[1] // 2
    gpad[:, :wide] = gsum[...].astype(BF16)
    gpad[:, wide:] = jnp.zeros((gpad.shape[0], 2 * half - wide), BF16)
    theirs = pl.ds(pl.multiple_of((1 - c) * half, half), half)
    ours = pl.ds(pl.multiple_of(c * half, half), half)
    send(gpad.at[:, theirs], pair_in, s_0, r_0, partner)
    wait_recv(pair_in, r_0, partner)
    shares[...] = (gpad[:, ours].astype(F32) + pair_in[...].astype(F32)).astype(BF16)

    block = 48

    def share(j, _):
        target, b = chip(j)
        send(shares.at[pl.ds(pl.multiple_of(b * block, 16), block)], r1.at[j], s_1.at[j], r_1.at[j], target)
        return 0

    lax.fori_loop(1, 8, share, 0)
    own = shares[pl.ds(pl.multiple_of((4 * zl + x) * block, 16), block), :].astype(F32)

    def take(j, total):
        wait_recv(r1.at[j], r_1.at[j], partner)
        return total + r1[j].astype(F32)

    own = lax.fori_loop(1, 8, take, own)
    mine_at = t * 4 + y
    r2[mine_at] = own.astype(BF16)

    def spread(j, _):
        target, b = group(j)
        send(r2.at[mine_at], r2.at[mine_at], s_2.at[b], r_2.at[mine_at], target)
        return 0

    lax.fori_loop(1, 8, spread, 0)

    def settle(b, _):
        @pl.when(b != mine_at)
        def _():
            wait_recv(r2.at[b], r_2.at[b], partner)

        return 0

    lax.fori_loop(0, 8, settle, 0)

    def add(b, total):
        return total + r2[b].astype(F32)

    fin[...] = lax.fori_loop(0, 8, add, jnp.zeros(fin.shape, F32)) * factor
    send(fin, fin_in, s_3, r_3, partner)
    wait_recv(fin_in, r_3, partner)

    @pl.when(c == 0)
    def _():
        grad[:, :half] = fin[:24, :]
        grad[:, half:] = fin_in[:24, : wide - half]

    @pl.when(c == 1)
    def _():
        grad[:, :half] = fin_in[24:, :]
        grad[:, half:] = fin[24:, : wide - half]

    def done(r, _):
        o = plane(r)[1]
        wait_send(flags, s_f.at[o], partner)
        wait_send(buf.at[pl.ds(pl.multiple_of(o * cap, cap), cap)], s_a.at[o], partner)
        return 0

    lax.fori_loop(1, owners, done, 0)

    def done_shares(j, _):
        target, b = chip(j)
        wait_send(shares.at[pl.ds(pl.multiple_of(b * block, 16), block)], s_1.at[j], partner)
        wait_send(r2.at[mine_at], s_2.at[group(j)[1]], partner)
        return 0

    lax.fori_loop(1, 8, done_shares, 0)
    wait_send(gpad.at[:, theirs], s_0, partner)
    wait_send(fin, s_3, partner)


def route(features, tokpos, counts, rows, head, factor, grad_rows):
    slots, width = rows.shape[0], features.shape[1]
    cap = slots // 32
    depth = rows.shape[1]
    half = 768
    dma = pltpu.SemaphoreType.DMA
    vmem = pl.BlockSpec(memory_space=pltpu.VMEM)
    return pl.pallas_call(
        functools.partial(route_kernel, factor, cap),
        out_shape=(
            jax.ShapeDtypeStruct((slots, width), BF16),
            jax.ShapeDtypeStruct((grad_rows, width), F32),
        ),
        in_specs=[vmem] * 5,
        out_specs=(vmem, vmem),
        scratch_shapes=[
            pltpu.VMEM((slots, width), BF16),
            pltpu.VMEM((slots, width), BF16),
            pltpu.VMEM((slots, width), F32),
            pltpu.VMEM((cap, 128), BF16),
            pltpu.VMEM((32, cap, 128), BF16),
            pltpu.VMEM((depth, width), F32),
            pltpu.VMEM((depth, 2 * half), BF16),
            pltpu.VMEM((depth, half), BF16),
            pltpu.VMEM((depth, half), BF16),
            pltpu.VMEM((8, 48, half), BF16),
            pltpu.VMEM((8, 48, half), BF16),
            pltpu.VMEM((48, half), F32),
            pltpu.VMEM((48, half), F32),
            dma((32,)), dma((32,)), dma((32,)), dma((32,)),
            dma, dma, dma((8,)), dma((8,)), dma((8,)), dma((8,)), dma, dma,
        ],
        compiler_params=pltpu.CompilerParams(
            collective_id=1, has_side_effects=True, vmem_limit_bytes=56 << 20
        ),
    )(features, tokpos, counts, rows, head)


def body(
    tokens, widen_weight, narrow_weight, head_weight, predictor_rows, target_index, destination
):
    owners = lax.axis_size("tgt") * lax.axis_size("fsdp")
    devices = owners * lax.axis_size("dp")
    normed = norm_rows(tokens.astype(F32)).astype(BF16)
    hidden = jax.nn.gelu(
        jnp.dot(
            normed,
            lax.all_gather(widen_weight, "fsdp", axis=1, tiled=True),
            preferred_element_type=F32,
        ),
        approximate=False,
    ).astype(BF16)
    branch = jnp.dot(
        hidden,
        lax.all_gather(narrow_weight, "fsdp", axis=1, tiled=True),
        preferred_element_type=F32,
    )
    features = norm_rows(tokens.astype(F32) + branch).astype(BF16)
    head = lax.all_gather(head_weight, "fsdp", axis=1, tiled=True)
    cap = predictor_rows.shape[0] // owners
    routed = destination[:, 0]
    entry = jnp.arange(routed.shape[0], dtype=jnp.int32)
    earlier = (routed[:, None] == routed[None, :]) & (entry[:, None] < entry[None, :])
    position = routed * cap + jnp.sum(earlier.astype(jnp.int32), axis=0)
    token = jnp.arange(tokens.shape[0], dtype=jnp.int32)
    chosen = target_index[:, None] == token[None, :]
    tokpos = jnp.sum(jnp.where(chosen, position[:, None] + 1, 0), axis=0)[None, :] - 1
    lane = jnp.arange(128, dtype=jnp.int32)
    counts = jnp.sum((routed[:, None] == lane[None, :]).astype(jnp.int32), axis=0)[None, :]
    factor = 1.0 / math.sqrt(target_index.shape[0] * devices)
    error, grad = route(
        features, tokpos, counts, predictor_rows, head, factor,
        predictor_rows.shape[1] // lax.axis_size("fsdp"),
    )
    return (features, error, grad)


def solution(mesh):
    in_specs = (
        P(("tgt", "fsdp", "dp"), None),
        P(None, "fsdp"),
        P(None, "fsdp"),
        P(None, "fsdp"),
        P(("tgt", "fsdp", "dp"), None),
        P(("tgt", "fsdp", "dp")),
        P(("tgt", "fsdp", "dp"), None),
    )
    out_specs = (P(("tgt", "fsdp", "dp"), None), P(("tgt", "fsdp", "dp"), None), P("fsdp", None))
    return jax.shard_map(body, mesh=mesh, in_specs=in_specs, out_specs=out_specs, check_vma=False)
```

```python
import functools
import math

import jax
import jax.numpy as jnp
from jax import lax
from jax.experimental import pallas as pl
from jax.experimental.pallas import tpu as pltpu
from jax.sharding import PartitionSpec as P

MESH = pl.DeviceIdType.MESH
F32, BF16 = jnp.float32, jnp.bfloat16


def norm_rows(values):
    center = jnp.mean(values, axis=-1, keepdims=True)
    shifted = values - center
    spread = jnp.mean(shifted * shifted, axis=-1, keepdims=True)
    return shifted * lax.rsqrt(spread + 1e-06)


def place():
    t, f, d = lax.axis_index("tgt"), lax.axis_index("fsdp"), lax.axis_index("dp")
    return lax.rem(f // 2, 4), d, 2 * t + f // 8, lax.rem(f, 2)


def device(x, y, z, c):
    return (z // 2, lax.rem(z, 2) * 8 + x * 2 + c, y)


def send(src, dst, send_sem, recv_sem, target):
    copy = pltpu.make_async_remote_copy(src, dst, send_sem, recv_sem, device_id=target, device_id_type=MESH)
    copy.start()


def wait_recv(dst, sem, target):
    pltpu.make_async_remote_copy(dst, dst, sem, sem, device_id=target, device_id_type=MESH).wait_recv()


def wait_send(src, sem, target):
    pltpu.make_async_remote_copy(src, src, sem, sem, device_id=target, device_id_type=MESH).wait_send()


def gelu(v):
    return 0.5 * v * (1.0 + lax.erf(v * math.sqrt(0.5)))


def encode_kernel(
    tokens, widen, narrow_t, head_t, feats, head_out,
    xs, w1, w2, hid, nar, nar_in, heads, kept, pp_out, pp_in, pc_out, pc_in, py_out, py_in, summed,
    s_xp, r_xp, s_xy, r_xy, s_xf, r_xf, s_wp, r_wp, s_wx, r_wx, s_wz, r_wz,
    s_np, r_np, s_nx, r_nx, s_nz, r_nz, s_hx, r_hx, s_hz, r_hz, s_hp, r_hp,
    s_pp, r_pp, s_pc, r_pc, s_py, r_py,
):
    x, y, z, c = place()
    zl, p = lax.rem(z, 2), lax.rem(y, 2)
    partner = device(x, y, z, 1 - c)
    y_up, y_down = lax.rem(y + 1, 4), lax.rem(y + 3, 4)
    z_up = device(x, y, lax.rem(z + 1, 4), c)
    z_down = device(x, y, lax.rem(z + 3, 4), c)
    ahead = lax.select(c == 0, y_up, y_down)
    behind = lax.select(c == 0, y_down, y_up)
    helper, helped = device(x, ahead, z, c), device(x, behind, z, c)
    steps, back = (0, 1, 3, 2), (0, 2, 1, 3)

    def at_x(step):
        return lax.rem(x + step, 4)

    def across(step):
        return device(at_x(step), y, z, c)

    ring = c == zl

    barrier = pltpu.get_barrier_semaphore()
    for other in (partner, helper, helped, z_up, z_down, across(1), across(2), across(3)):
        pl.semaphore_signal(barrier, inc=1, device_id=other, device_id_type=MESH)

    xs[0] = norm_rows(tokens[...].astype(F32)).astype(BF16)
    for group in range(2):
        for k in range(4):
            unit = (8 * group + 2 * k + p) * 384
            nar[group, :88, 384 * k : 384 * (k + 1)] = narrow_t[:, pl.ds(pl.multiple_of(unit, 384), 384)]
    nar[:, 88:, :] = jnp.zeros((2, 8, 1536), BF16)
    heads[zl, x, c, :88, :] = head_t[...]
    heads[zl, x, c, 88:, :] = jnp.zeros((8, 384), BF16)
    w2[0, 704:, :] = jnp.zeros((64, 1536), BF16)
    w2[1, :64, :] = jnp.zeros((64, 1536), BF16)
    pl.semaphore_wait(barrier, 8)

    def spread_z(at):
        send(w1.at[at, pl.ds(0, 704)], w1.at[at, pl.ds(0, 704)], s_wz.at[at, 0], r_wz.at[at, 0], z_up)
        send(w1.at[at, pl.ds(704, 704)], w1.at[at, pl.ds(704, 704)], s_wz.at[at, 1], r_wz.at[at, 1], z_down)

    def spread_x():
        for k in (1, 2, 3):
            send(w1.at[x], w1.at[x], s_wx.at[k], r_wx.at[back[k]], across(steps[k]))

    @pl.when((c == p) & (c != zl))
    def _():
        send(widen, w1.at[x], s_wp, r_wp, partner)

    send(xs.at[0], xs.at[2 + c], s_xy, r_xy, helper)

    @pl.when((c == p) & ring)
    def _():
        w1[x] = widen[...]
        spread_x()
        spread_z(x)

    send(xs.at[0], xs.at[1], s_xp, r_xp, partner)
    send(nar.at[1 - c], nar_in, s_np, r_np, partner)

    @pl.when((c != p) & ring)
    def _():
        wait_recv(w1.at[x], r_wp, partner)
        spread_x()
        spread_z(x)

    def hidden(slot, at):
        block = jnp.dot(xs[slot], w1[at], preferred_element_type=F32)
        hid[slot, :, pl.ds(pl.multiple_of(at * 384, 384), 384)] = gelu(block).astype(BF16)

    def piece(side, at):
        return pl.multiple_of(64 * side + 176 * at, 16)

    def spread_narrow_z(at):
        row = piece(zl, at)
        upper, lower = w2.at[zl, pl.ds(row, 96)], w2.at[zl, pl.ds(row + 96, 80)]
        send(upper, upper, s_nz.at[at, 0], r_nz.at[at, 0], z_up)
        send(lower, lower, s_nz.at[at, 1], r_nz.at[at, 1], z_down)

    def spread_head_z(at):
        src = heads.at[zl, at, c]

        @pl.when(lax.rem(at, 2) == 0)
        def _():
            send(src, src, s_hz.at[at], r_hz.at[at], z_up)

        @pl.when(lax.rem(at, 2) == 1)
        def _():
            send(src, src, s_hz.at[at], r_hz.at[at], z_down)

    def arrive_widen(k):
        at = at_x(steps[k])
        if k:
            @pl.when(ring)
            def _():
                wait_recv(w1.at[at], r_wx.at[k], partner)
                spread_z(at)

        @pl.when(jnp.logical_not(ring))
        def _():
            wait_recv(w1.at[at, pl.ds(0, 704)], r_wz.at[at, 0], partner)
            wait_recv(w1.at[at, pl.ds(704, 704)], r_wz.at[at, 1], partner)

        return at

    wait_recv(nar_in, r_np, partner)
    mine, other = nar[c, :88, :].astype(F32), nar_in[:88, :].astype(F32)
    row = piece(zl, x)

    @pl.when(c == 0)
    def _():
        w2[zl, pl.ds(row, 176), :] = jnp.concatenate([mine, other], axis=0).astype(BF16)

    @pl.when(c == 1)
    def _():
        w2[zl, pl.ds(row, 176), :] = jnp.concatenate([other, mine], axis=0).astype(BF16)

    spread_narrow_z(x)
    at = arrive_widen(0)
    hidden(0, at)
    wait_recv(xs.at[1], r_xp, partner)
    hidden(1, at)
    own = w2.at[zl, pl.ds(row, 176)]
    for k in (1, 2, 3):
        send(own, own, s_nx.at[k], r_nx.at[back[k]], across(steps[k]))
    own_head = heads.at[zl, x, c]
    for k in (1, 2, 3):
        send(own_head, own_head, s_hx.at[k], r_hx.at[back[k]], across(steps[k]))
    wait_recv(xs.at[2 + c], r_xy, partner)
    send(xs.at[2 + c], xs.at[2 + c], s_xf, r_xf, partner)
    hidden(2 + c, at)
    wait_recv(xs.at[3 - c], r_xf, partner)
    hidden(3 - c, at)
    spread_head_z(x)

    for k in (1, 2, 3):
        at = arrive_widen(k)

        def fill(slot, _):
            hidden(slot, at)
            return 0

        lax.fori_loop(0, 4, fill, 0)

    for k in (1, 2, 3):
        at = at_x(steps[k])
        wait_recv(w2.at[zl, pl.ds(piece(zl, at), 176)], r_nx.at[k], partner)
        spread_narrow_z(at)
    for k in (1, 2, 3):
        at = at_x(steps[k])
        wait_recv(heads.at[zl, at, c], r_hx.at[k], partner)
        spread_head_z(at)

    def partial(slot, side):
        return lax.dot_general(
            hid[slot], w2[side], (((1,), (1,)), ((), ())), preferred_element_type=F32
        )

    def add(value, side):
        @pl.when(side == 0)
        def _():
            summed[:, :768] += value

        @pl.when(side == 1)
        def _():
            summed[:, 640:] += value

    summed[...] = tokens[...].astype(F32)
    for turn in range(2):
        side = zl if turn == 0 else 1 - zl
        if turn == 1:
            for k in range(4):
                row = piece(side, at_x(steps[k]))
                at = at_x(steps[k])
                wait_recv(w2.at[side, pl.ds(row, 96)], r_nz.at[at, 0], partner)
                wait_recv(w2.at[side, pl.ds(row + 96, 80)], r_nz.at[at, 1], partner)
        pc_out[turn] = partial(3 - c, side).astype(BF16)
        send(pc_out.at[turn], pc_in.at[turn], s_pc.at[turn], r_pc.at[turn], partner)
        kept[...] = partial(2 + c, side)
        wait_recv(pc_in.at[turn], r_pc.at[turn], partner)
        py_out[turn] = (kept[...] + pc_in[turn].astype(F32)).astype(BF16)
        send(py_out.at[turn], py_in.at[turn], s_py.at[turn], r_py.at[turn], helped)
        pp_out[turn] = partial(1, side).astype(BF16)
        send(pp_out.at[turn], pp_in.at[turn], s_pp.at[turn], r_pp.at[turn], partner)
        add(partial(0, side), side)

    for k in range(4):
        at = at_x(steps[k])
        wait_recv(heads.at[1 - zl, at, c], r_hz.at[at], partner)
    send(heads.at[:, :, c], heads.at[:, :, c], s_hp, r_hp, partner)
    for turn in range(2):
        side = zl if turn == 0 else 1 - zl
        wait_recv(pp_in.at[turn], r_pp.at[turn], partner)
        add(pp_in[turn].astype(F32), side)
        if turn == 1:
            wait_recv(heads.at[:, :, 1 - c], r_hp, partner)
            for k in range(8):
                both = [heads[k // 4, k % 4, core, :88, :].astype(F32) for core in range(2)]
                head_out[k] = jnp.concatenate(both, axis=0).astype(BF16)
        wait_recv(py_in.at[turn], r_py.at[turn], partner)
        add(py_in[turn].astype(F32), side)
    feats[...] = norm_rows(summed[...]).astype(BF16)

    @pl.when((c == p) & (c != zl))
    def _():
        wait_send(widen, s_wp, partner)

    wait_send(xs.at[0], s_xy, partner)
    wait_send(xs.at[0], s_xp, partner)
    wait_send(xs.at[2 + c], s_xf, partner)
    wait_send(nar.at[1 - c], s_np, partner)
    wait_send(heads.at[:, :, c], s_hp, partner)
    for k in range(4):
        at = at_x(steps[k])
        row = piece(zl, at)

        @pl.when(ring)
        def _():
            if k:
                wait_send(w1.at[x], s_wx.at[k], partner)
            wait_send(w1.at[at, pl.ds(0, 704)], s_wz.at[at, 0], partner)
            wait_send(w1.at[at, pl.ds(704, 704)], s_wz.at[at, 1], partner)

        if k:
            wait_send(own, s_nx.at[k], partner)
            wait_send(own_head, s_hx.at[k], partner)
        wait_send(w2.at[zl, pl.ds(row, 96)], s_nz.at[at, 0], partner)
        wait_send(w2.at[zl, pl.ds(row + 96, 80)], s_nz.at[at, 1], partner)
        wait_send(heads.at[zl, at, c], s_hz.at[at], partner)
    for turn in range(2):
        wait_send(pc_out.at[turn], s_pc.at[turn], partner)
        wait_send(py_out.at[turn], s_py.at[turn], partner)
        wait_send(pp_out.at[turn], s_pp.at[turn], partner)


def encode(tokens, widen_weight, narrow_weight, head_weight):
    rows, width = tokens.shape
    dma = pltpu.SemaphoreType.DMA
    vmem = pl.BlockSpec(memory_space=pltpu.VMEM)
    part = pltpu.VMEM((2, rows, 768), BF16)
    return pl.pallas_call(
        encode_kernel,
        out_shape=(
            jax.ShapeDtypeStruct((rows, width), BF16),
            jax.ShapeDtypeStruct((8, 176, 384), BF16),
        ),
        in_specs=[vmem] * 4,
        out_specs=(vmem, vmem),
        scratch_shapes=[
            pltpu.VMEM((4, rows, width), BF16),
            pltpu.VMEM((4, width, 384), BF16),
            pltpu.VMEM((2, 768, 1536), BF16),
            pltpu.VMEM((4, rows, 1536), BF16),
            pltpu.VMEM((2, 96, 1536), BF16),
            pltpu.VMEM((96, 1536), BF16),
            pltpu.VMEM((2, 4, 2, 96, 384), BF16),
            pltpu.VMEM((rows, 768), F32),
            part, part, part, part, part, part,
            pltpu.VMEM((rows, width), F32),
            dma, dma, dma, dma, dma, dma, dma, dma, dma((4,)), dma((4,)), dma((4, 2)), dma((4, 2)),
            dma, dma, dma((4,)), dma((4,)), dma((4, 2)), dma((4, 2)),
            dma((4,)), dma((4,)), dma((4,)), dma((4,)), dma, dma,
            dma((2,)), dma((2,)), dma((2,)), dma((2,)), dma((2,)), dma((2,)),
        ],
        compiler_params=pltpu.CompilerParams(
            collective_id=2, has_side_effects=True, vmem_limit_bytes=56 << 20
        ),
    )(tokens, widen_weight, narrow_weight.T, head_weight.T)


def route_kernel(
    factor, cap, feat, tokpos, counts, rows, head, error, grad,
    buf, rcv, pred, flags, flags_in, gsum, gpad, pair_in, shares, r1, r2, fin, fin_in,
    s_a, r_a, s_f, r_f, s_0, r_0, s_1, r_1, s_2, r_2, s_3, r_3,
):
    x, y, z, c = place()
    t, zl = z // 2, lax.rem(z, 2)
    me = 8 * z + 2 * x + c
    owners = 32

    def plane(r):
        nx, nz, nc = lax.rem(x + lax.rem(r // 2, 4), 4), lax.rem(z + r // 8, 4), lax.rem(c + lax.rem(r, 2), 2)
        return device(nx, y, nz, nc), 8 * nz + 2 * nx + nc

    def plane_from(r):
        nx = lax.rem(x + 4 - lax.rem(r // 2, 4), 4)
        nz, nc = lax.rem(z + 4 - r // 8, 4), lax.rem(c + lax.rem(r, 2), 2)
        return device(nx, y, nz, nc), 8 * nz + 2 * nx + nc

    def group(j):
        nt, nd = lax.rem(t + j // 4, 2), lax.rem(y + lax.rem(j, 4), 4)
        return device(x, nd, 2 * nt + zl, c), nt * 4 + nd

    def chip(j):
        nz, nx = lax.rem(zl + j // 4, 2), lax.rem(x + lax.rem(j, 4), 4)
        return device(nx, y, 2 * t + nz, c), 4 * nz + nx

    partner = device(x, y, z, 1 - c)

    barrier = pltpu.get_barrier_semaphore()

    def greet(r, _):
        pl.semaphore_signal(barrier, inc=1, device_id=plane(r)[0], device_id_type=MESH)
        return 0

    lax.fori_loop(1, owners, greet, 0)

    def greet_group(j, _):
        @pl.when(lax.rem(j, 4) != 0)
        def _():
            pl.semaphore_signal(barrier, inc=1, device_id=group(j)[0], device_id_type=MESH)

        return 0

    lax.fori_loop(1, 8, greet_group, 0)

    slot_row = lax.broadcasted_iota(jnp.int32, (cap, 128), 0)
    flags[...] = jnp.where(slot_row < counts[...], 1.0, 0.0).astype(BF16)

    def fill(i, _):
        rows_at = pl.ds(pl.multiple_of(i * 128, 128), 128)
        slot = lax.broadcasted_iota(jnp.int32, (128, feat.shape[0]), 0) + i * 128
        pick = jnp.where(slot == tokpos[...], 1.0, 0.0).astype(BF16)
        buf[rows_at, :] = jnp.dot(pick, feat[...], preferred_element_type=F32).astype(BF16)
        return 0

    lax.fori_loop(0, owners * cap // 128, fill, 0)

    pl.semaphore_wait(barrier, owners - 1 + 6)

    def out(r, _):
        target, o = plane(r)
        send(flags, flags_in.at[me], s_f.at[o], r_f.at[me], target)
        src = buf.at[pl.ds(pl.multiple_of(o * cap, cap), cap)]
        send(src, rcv.at[pl.ds(pl.multiple_of(me * cap, cap), cap)], s_a.at[o], r_a.at[me], target)
        return 0

    lax.fori_loop(1, owners, out, 0)
    mine = pl.ds(pl.multiple_of(me * cap, cap), cap)
    rcv[mine, :] = buf[mine, :]
    flags_in[me] = flags[...]

    def predict(i, _):
        rows_at = pl.ds(pl.multiple_of(i * 128, 128), 128)
        pred[rows_at, :] = lax.dot_general(
            rows[rows_at, :], head[...], (((1,), (1,)), ((), ())), preferred_element_type=F32
        )
        return 0

    lax.fori_loop(0, owners * cap // 128, predict, 0)
    gsum[...] = jnp.zeros_like(gsum)

    per = 8

    def arrive(k, _):
        i = lax.rem(z + k, 4)

        def one(q, _):
            s = i * per + q

            @pl.when(s != me)
            def _():
                wait_recv(flags_in.at[s], r_f.at[s], partner)
                wait_recv(rcv.at[pl.ds(pl.multiple_of(s * cap, cap), cap)], r_a.at[s], partner)

            return 0

        lax.fori_loop(0, per, one, 0)
        rows_at = pl.ds(pl.multiple_of(i * (per * cap), per * cap), per * cap)
        lane = lax.broadcasted_iota(jnp.int32, (per * cap, 128), 1)
        live = flags_in[pl.ds(i * per, per)].astype(F32).reshape(per * cap, 128)
        live = jnp.sum(jnp.where(lane == me, live, 0.0), axis=1, keepdims=True)
        wrong = jnp.where(live > 0.5, pred[rows_at, :] - rcv[rows_at, :].astype(F32), 0.0).astype(BF16)
        error[rows_at, :] = wrong
        gsum[...] += lax.dot_general(
            rows[rows_at, :], wrong, (((0,), (0,)), ((), ())), preferred_element_type=F32
        )
        return 0

    lax.fori_loop(0, 4, arrive, 0)

    wide = gsum.shape[1]
    half = gpad.shape[1] // 2
    gpad[:, :wide] = gsum[...].astype(BF16)
    gpad[:, wide:] = jnp.zeros((gpad.shape[0], 2 * half - wide), BF16)
    theirs = pl.ds(pl.multiple_of((1 - c) * half, half), half)
    ours = pl.ds(pl.multiple_of(c * half, half), half)
    send(gpad.at[:, theirs], pair_in, s_0, r_0, partner)
    wait_recv(pair_in, r_0, partner)
    shares[...] = (gpad[:, ours].astype(F32) + pair_in[...].astype(F32)).astype(BF16)

    block = 48

    def share(j, _):
        target, b = chip(j)
        send(shares.at[pl.ds(pl.multiple_of(b * block, 16), block)], r1.at[j], s_1.at[j], r_1.at[j], target)
        return 0

    lax.fori_loop(1, 8, share, 0)
    own = shares[pl.ds(pl.multiple_of((4 * zl + x) * block, 16), block), :].astype(F32)

    def take(j, total):
        wait_recv(r1.at[j], r_1.at[j], partner)
        return total + r1[j].astype(F32)

    own = lax.fori_loop(1, 8, take, own)
    mine_at = t * 4 + y
    r2[mine_at] = own.astype(BF16)

    def spread(j, _):
        target, b = group(j)
        send(r2.at[mine_at], r2.at[mine_at], s_2.at[b], r_2.at[mine_at], target)
        return 0

    lax.fori_loop(1, 8, spread, 0)

    def settle(b, _):
        @pl.when(b != mine_at)
        def _():
            wait_recv(r2.at[b], r_2.at[b], partner)

        return 0

    lax.fori_loop(0, 8, settle, 0)

    def add(b, total):
        return total + r2[b].astype(F32)

    fin[...] = lax.fori_loop(0, 8, add, jnp.zeros(fin.shape, F32)) * factor
    send(fin, fin_in, s_3, r_3, partner)
    wait_recv(fin_in, r_3, partner)

    @pl.when(c == 0)
    def _():
        grad[:, :half] = fin[:24, :]
        grad[:, half:] = fin_in[:24, : wide - half]

    @pl.when(c == 1)
    def _():
        grad[:, :half] = fin_in[24:, :]
        grad[:, half:] = fin[24:, : wide - half]

    def done(r, _):
        o = plane(r)[1]
        wait_send(flags, s_f.at[o], partner)
        wait_send(buf.at[pl.ds(pl.multiple_of(o * cap, cap), cap)], s_a.at[o], partner)
        return 0

    lax.fori_loop(1, owners, done, 0)

    def done_shares(j, _):
        target, b = chip(j)
        wait_send(shares.at[pl.ds(pl.multiple_of(b * block, 16), block)], s_1.at[j], partner)
        wait_send(r2.at[mine_at], s_2.at[group(j)[1]], partner)
        return 0

    lax.fori_loop(1, 8, done_shares, 0)
    wait_send(gpad.at[:, theirs], s_0, partner)
    wait_send(fin, s_3, partner)


def route(features, tokpos, counts, rows, head, factor, grad_rows):
    slots, width = rows.shape[0], features.shape[1]
    cap = slots // 32
    depth = rows.shape[1]
    half = 768
    dma = pltpu.SemaphoreType.DMA
    vmem = pl.BlockSpec(memory_space=pltpu.VMEM)
    return pl.pallas_call(
        functools.partial(route_kernel, factor, cap),
        out_shape=(
            jax.ShapeDtypeStruct((slots, width), BF16),
            jax.ShapeDtypeStruct((grad_rows, width), F32),
        ),
        in_specs=[vmem] * 5,
        out_specs=(vmem, vmem),
        scratch_shapes=[
            pltpu.VMEM((slots, width), BF16),
            pltpu.VMEM((slots, width), BF16),
            pltpu.VMEM((slots, width), F32),
            pltpu.VMEM((cap, 128), BF16),
            pltpu.VMEM((32, cap, 128), BF16),
            pltpu.VMEM((depth, width), F32),
            pltpu.VMEM((depth, 2 * half), BF16),
            pltpu.VMEM((depth, half), BF16),
            pltpu.VMEM((depth, half), BF16),
            pltpu.VMEM((8, 48, half), BF16),
            pltpu.VMEM((8, 48, half), BF16),
            pltpu.VMEM((48, half), F32),
            pltpu.VMEM((48, half), F32),
            dma((32,)), dma((32,)), dma((32,)), dma((32,)),
            dma, dma, dma((8,)), dma((8,)), dma((8,)), dma((8,)), dma, dma,
        ],
        compiler_params=pltpu.CompilerParams(
            collective_id=1, has_side_effects=True, vmem_limit_bytes=56 << 20
        ),
    )(features, tokpos, counts, rows, head)


def body(
    tokens, widen_weight, narrow_weight, head_weight, predictor_rows, target_index, destination
):
    owners = lax.axis_size("tgt") * lax.axis_size("fsdp")
    devices = owners * lax.axis_size("dp")
    features, head = encode(tokens, widen_weight, narrow_weight, head_weight)
    head = head.reshape(features.shape[1], predictor_rows.shape[1])
    cap = predictor_rows.shape[0] // owners
    routed = destination[:, 0]
    entry = jnp.arange(routed.shape[0], dtype=jnp.int32)
    earlier = (routed[:, None] == routed[None, :]) & (entry[:, None] < entry[None, :])
    position = routed * cap + jnp.sum(earlier.astype(jnp.int32), axis=0)
    token = jnp.arange(tokens.shape[0], dtype=jnp.int32)
    chosen = target_index[:, None] == token[None, :]
    tokpos = jnp.sum(jnp.where(chosen, position[:, None] + 1, 0), axis=0)[None, :] - 1
    lane = jnp.arange(128, dtype=jnp.int32)
    counts = jnp.sum((routed[:, None] == lane[None, :]).astype(jnp.int32), axis=0)[None, :]
    factor = 1.0 / math.sqrt(target_index.shape[0] * devices)
    error, grad = route(
        features, tokpos, counts, predictor_rows, head, factor,
        predictor_rows.shape[1] // lax.axis_size("fsdp"),
    )
    return (features, error, grad)


def solution(mesh):
    in_specs = (
        P(("tgt", "fsdp", "dp"), None),
        P(None, "fsdp"),
        P(None, "fsdp"),
        P(None, "fsdp"),
        P(("tgt", "fsdp", "dp"), None),
        P(("tgt", "fsdp", "dp")),
        P(("tgt", "fsdp", "dp"), None),
    )
    out_specs = (P(("tgt", "fsdp", "dp"), None), P(("tgt", "fsdp", "dp"), None), P("fsdp", None))
    return jax.shard_map(body, mesh=mesh, in_specs=in_specs, out_specs=out_specs, check_vma=False)
```

```python
import functools
import math

import jax
import jax.numpy as jnp
from jax import lax
from jax.experimental import pallas as pl
from jax.experimental.pallas import tpu as pltpu
from jax.sharding import PartitionSpec as P

MESH = pl.DeviceIdType.MESH
F32, BF16 = jnp.float32, jnp.bfloat16


def norm_rows(values):
    center = jnp.mean(values, axis=-1, keepdims=True)
    shifted = values - center
    spread = jnp.mean(shifted * shifted, axis=-1, keepdims=True)
    return shifted * lax.rsqrt(spread + 1e-06)


def place():
    t, f, d = lax.axis_index("tgt"), lax.axis_index("fsdp"), lax.axis_index("dp")
    return lax.rem(f // 2, 4), d, 2 * t + f // 8, lax.rem(f, 2)


def device(x, y, z, c):
    return (z // 2, lax.rem(z, 2) * 8 + x * 2 + c, y)


def send(src, dst, send_sem, recv_sem, target):
    copy = pltpu.make_async_remote_copy(src, dst, send_sem, recv_sem, device_id=target, device_id_type=MESH)
    copy.start()


def wait_recv(dst, sem, target):
    pltpu.make_async_remote_copy(dst, dst, sem, sem, device_id=target, device_id_type=MESH).wait_recv()


def wait_send(src, sem, target):
    pltpu.make_async_remote_copy(src, src, sem, sem, device_id=target, device_id_type=MESH).wait_send()


def gelu(v):
    return 0.5 * v * (1.0 + lax.erf(v * math.sqrt(0.5)))


def encode_kernel(
    tokens, widen, narrow_t, head_t, feats, head_out,
    xs, w1, w2, hid, nar, nar_in, heads, kept, pp_out, pp_in, pc_out, pc_in, py_out, py_in, summed,
    s_xp, r_xp, s_xy, r_xy, s_xf, r_xf, s_wp, r_wp, s_wx, r_wx, s_wz, r_wz,
    s_np, r_np, s_nx, r_nx, s_nz, r_nz, s_hx, r_hx, s_hz, r_hz, s_hp, r_hp,
    s_pp, r_pp, s_pc, r_pc, s_py, r_py, s_wf, r_wf, s_nf, r_nf,
):
    x, y, z, c = place()
    zl, p = lax.rem(z, 2), lax.rem(y, 2)
    partner = device(x, y, z, 1 - c)
    y_up, y_down = lax.rem(y + 1, 4), lax.rem(y + 3, 4)
    z_up = device(x, y, lax.rem(z + 1, 4), c)
    z_down = device(x, y, lax.rem(z + 3, 4), c)
    ahead = lax.select(c == 0, y_up, y_down)
    behind = lax.select(c == 0, y_down, y_up)
    helper, helped = device(x, ahead, z, c), device(x, behind, z, c)
    steps, back = (0, 1, 3, 2), (0, 2, 1, 3)

    def at_x(step):
        return lax.rem(x + step, 4)

    def across(step):
        return device(at_x(step), y, z, c)

    ring = c == zl

    barrier = pltpu.get_barrier_semaphore()
    for other in (partner, helper, helped, z_up, z_down, across(1), across(2), across(3)):
        pl.semaphore_signal(barrier, inc=1, device_id=other, device_id_type=MESH)

    xs[0] = norm_rows(tokens[...].astype(F32)).astype(BF16)
    for group in range(2):
        for k in range(4):
            unit = (8 * group + 2 * k + p) * 384
            nar[group, :88, 384 * k : 384 * (k + 1)] = narrow_t[:, pl.ds(pl.multiple_of(unit, 384), 384)]
    nar[:, 88:, :] = jnp.zeros((2, 8, 1536), BF16)
    heads[zl, x, c, :88, :] = head_t[...]
    heads[zl, x, c, 88:, :] = jnp.zeros((8, 384), BF16)
    w2[0, 704:, :] = jnp.zeros((64, 1536), BF16)
    w2[1, :64, :] = jnp.zeros((64, 1536), BF16)
    pl.semaphore_wait(barrier, 8)

    def spread_z(at):
        send(w1.at[at, pl.ds(0, 704)], w1.at[at, pl.ds(0, 704)], s_wz.at[at, 0], r_wz.at[at, 0], z_up)
        send(w1.at[at, pl.ds(704, 704)], w1.at[at, pl.ds(704, 704)], s_wz.at[at, 1], r_wz.at[at, 1], z_down)

    def spread_x():
        for k in (1, 2):
            send(w1.at[x], w1.at[x], s_wx.at[k], r_wx.at[back[k]], across(steps[k]))

    def pass_x(at, k):
        half = w1.at[at, pl.ds(0, 704)] if k == 2 else w1.at[at, pl.ds(704, 704)]
        send(half, half, s_wf.at[k], r_wf.at[k], across(4 - steps[k]))

    @pl.when((c == p) & (c != zl))
    def _():
        send(widen, w1.at[x], s_wp, r_wp, partner)

    send(nar.at[1 - c], nar_in, s_np, r_np, partner)
    send(xs.at[0], xs.at[2 + c], s_xy, r_xy, helper)

    @pl.when((c == p) & ring)
    def _():
        w1[x] = widen[...]
        spread_x()
        spread_z(x)

    send(xs.at[0], xs.at[1], s_xp, r_xp, partner)

    @pl.when((c != p) & ring)
    def _():
        wait_recv(w1.at[x], r_wp, partner)
        spread_x()
        spread_z(x)

    def hidden(slot, at):
        block = jnp.dot(xs[slot], w1[at], preferred_element_type=F32)
        hid[slot, :, pl.ds(pl.multiple_of(at * 384, 384), 384)] = gelu(block).astype(BF16)

    def all_hidden(at):
        def fill(slot, _):
            hidden(slot, at)
            return 0

        lax.fori_loop(0, 4, fill, 0)

    def piece(side, at):
        return pl.multiple_of(64 * side + 176 * at, 16)

    def upper(side, at):
        return w2.at[side, pl.ds(piece(side, at), 96)]

    def lower(side, at):
        return w2.at[side, pl.ds(pl.multiple_of(piece(side, at) + 96, 16), 80)]

    def spread_narrow_z(at):
        send(upper(zl, at), upper(zl, at), s_nz.at[at, 0], r_nz.at[at, 0], z_up)
        send(lower(zl, at), lower(zl, at), s_nz.at[at, 1], r_nz.at[at, 1], z_down)

    own = w2.at[zl, pl.ds(piece(zl, x), 176)]
    own_head = heads.at[zl, x, c]

    def spread_narrow_x():
        for k in (1, 2):
            send(own, own, s_nx.at[k], r_nx.at[back[k]], across(steps[k]))

    def spread_head_x():
        for k in (1, 2, 3):
            send(own_head, own_head, s_hx.at[k], r_hx.at[back[k]], across(steps[k]))

    def spread_head_z(at):
        src = heads.at[zl, at, c]

        @pl.when(lax.rem(at, 2) == 0)
        def _():
            send(src, src, s_hz.at[at], r_hz.at[at], z_up)

        @pl.when(lax.rem(at, 2) == 1)
        def _():
            send(src, src, s_hz.at[at], r_hz.at[at], z_down)

    def widen_near():
        for k in (1, 2):
            at = at_x(steps[k])
            wait_recv(w1.at[at], r_wx.at[k], partner)
            pass_x(at, k)
            spread_z(at)

    def widen_far():
        at = at_x(2)
        wait_recv(w1.at[at, pl.ds(0, 704)], r_wf.at[2], partner)
        wait_recv(w1.at[at, pl.ds(704, 704)], r_wf.at[1], partner)
        spread_z(at)

    def widen_z(at):
        wait_recv(w1.at[at, pl.ds(0, 704)], r_wz.at[at, 0], partner)
        wait_recv(w1.at[at, pl.ds(704, 704)], r_wz.at[at, 1], partner)

    def narrow_near():
        for k in (1, 2):
            at = at_x(steps[k])
            wait_recv(w2.at[zl, pl.ds(piece(zl, at), 176)], r_nx.at[k], partner)
            half = (upper if k == 2 else lower)(zl, at)
            send(half, half, s_nf.at[k], r_nf.at[k], across(4 - steps[k]))
            spread_narrow_z(at)

    def narrow_far():
        at = at_x(2)
        wait_recv(upper(zl, at), r_nf.at[2], partner)
        wait_recv(lower(zl, at), r_nf.at[1], partner)
        spread_narrow_z(at)

    def neighbour_rows(at):
        wait_recv(xs.at[2 + c], r_xy, partner)
        send(xs.at[2 + c], xs.at[2 + c], s_xf, r_xf, partner)
        hidden(2 + c, at)
        wait_recv(xs.at[3 - c], r_xf, partner)
        hidden(3 - c, at)

    wait_recv(nar_in, r_np, partner)
    mine, other = nar[c, :88, :].astype(F32), nar_in[:88, :].astype(F32)

    @pl.when(c == 0)
    def _():
        own[...] = jnp.concatenate([mine, other], axis=0).astype(BF16)

    @pl.when(c == 1)
    def _():
        own[...] = jnp.concatenate([other, mine], axis=0).astype(BF16)

    spread_narrow_z(x)

    @pl.when(ring)
    def _():
        hidden(0, x)
        wait_recv(xs.at[1], r_xp, partner)
        hidden(1, x)
        widen_near()
        spread_narrow_x()
        spread_head_x()
        spread_head_z(x)
        neighbour_rows(x)
        all_hidden(at_x(1))
        widen_far()
        all_hidden(at_x(3))
        narrow_near()
        all_hidden(at_x(2))
        narrow_far()

    @pl.when(jnp.logical_not(ring))
    def _():
        spread_narrow_x()
        widen_z(x)
        hidden(0, x)
        wait_recv(xs.at[1], r_xp, partner)
        hidden(1, x)
        narrow_near()
        spread_head_x()
        spread_head_z(x)
        neighbour_rows(x)
        narrow_far()
        for k in (1, 2, 3):
            widen_z(at_x(steps[k]))
            all_hidden(at_x(steps[k]))

    for k in (1, 2, 3):
        at = at_x(steps[k])
        wait_recv(heads.at[zl, at, c], r_hx.at[k], partner)
        spread_head_z(at)

    def partial(slot, side):
        return lax.dot_general(
            hid[slot], w2[side], (((1,), (1,)), ((), ())), preferred_element_type=F32
        )

    def add(value, side):
        @pl.when(side == 0)
        def _():
            summed[:, :768] += value

        @pl.when(side == 1)
        def _():
            summed[:, 640:] += value

    summed[...] = tokens[...].astype(F32)
    for turn in range(2):
        side = zl if turn == 0 else 1 - zl
        if turn == 1:
            for k in range(4):
                at = at_x(steps[k])
                wait_recv(upper(side, at), r_nz.at[at, 0], partner)
                wait_recv(lower(side, at), r_nz.at[at, 1], partner)
        pc_out[turn] = partial(3 - c, side).astype(BF16)
        send(pc_out.at[turn], pc_in.at[turn], s_pc.at[turn], r_pc.at[turn], partner)
        kept[...] = partial(2 + c, side)
        wait_recv(pc_in.at[turn], r_pc.at[turn], partner)
        py_out[turn] = (kept[...] + pc_in[turn].astype(F32)).astype(BF16)
        send(py_out.at[turn], py_in.at[turn], s_py.at[turn], r_py.at[turn], helped)
        pp_out[turn] = partial(1, side).astype(BF16)
        send(pp_out.at[turn], pp_in.at[turn], s_pp.at[turn], r_pp.at[turn], partner)
        add(partial(0, side), side)

    for k in range(4):
        at = at_x(steps[k])
        wait_recv(heads.at[1 - zl, at, c], r_hz.at[at], partner)
    send(heads.at[:, :, c], heads.at[:, :, c], s_hp, r_hp, partner)
    for turn in range(2):
        side = zl if turn == 0 else 1 - zl
        wait_recv(pp_in.at[turn], r_pp.at[turn], partner)
        add(pp_in[turn].astype(F32), side)
        if turn == 1:
            wait_recv(heads.at[:, :, 1 - c], r_hp, partner)
            for k in range(8):
                both = [heads[k // 4, k % 4, core, :88, :].astype(F32) for core in range(2)]
                head_out[k] = jnp.concatenate(both, axis=0).astype(BF16)
        wait_recv(py_in.at[turn], r_py.at[turn], partner)
        add(py_in[turn].astype(F32), side)
    feats[...] = norm_rows(summed[...]).astype(BF16)

    @pl.when((c == p) & (c != zl))
    def _():
        wait_send(widen, s_wp, partner)

    wait_send(xs.at[0], s_xy, partner)
    wait_send(xs.at[0], s_xp, partner)
    wait_send(xs.at[2 + c], s_xf, partner)
    wait_send(nar.at[1 - c], s_np, partner)
    wait_send(heads.at[:, :, c], s_hp, partner)
    for k in range(4):
        at = at_x(steps[k])

        @pl.when(ring)
        def _():
            if k in (1, 2):
                wait_send(w1.at[x], s_wx.at[k], partner)
                wait_send(w1.at[x, pl.ds(0, 704)], s_wf.at[k], partner)
            wait_send(w1.at[at, pl.ds(0, 704)], s_wz.at[at, 0], partner)
            wait_send(w1.at[at, pl.ds(704, 704)], s_wz.at[at, 1], partner)

        if k in (1, 2):
            wait_send(own, s_nx.at[k], partner)
            wait_send((upper if k == 2 else lower)(zl, x), s_nf.at[k], partner)
        if k:
            wait_send(own_head, s_hx.at[k], partner)
        wait_send(upper(zl, at), s_nz.at[at, 0], partner)
        wait_send(lower(zl, at), s_nz.at[at, 1], partner)
        wait_send(heads.at[zl, at, c], s_hz.at[at], partner)
    for turn in range(2):
        wait_send(pc_out.at[turn], s_pc.at[turn], partner)
        wait_send(py_out.at[turn], s_py.at[turn], partner)
        wait_send(pp_out.at[turn], s_pp.at[turn], partner)


def encode(tokens, widen_weight, narrow_weight, head_weight):
    rows, width = tokens.shape
    dma = pltpu.SemaphoreType.DMA
    vmem = pl.BlockSpec(memory_space=pltpu.VMEM)
    part = pltpu.VMEM((2, rows, 768), BF16)
    return pl.pallas_call(
        encode_kernel,
        out_shape=(
            jax.ShapeDtypeStruct((rows, width), BF16),
            jax.ShapeDtypeStruct((8, 176, 384), BF16),
        ),
        in_specs=[vmem] * 4,
        out_specs=(vmem, vmem),
        scratch_shapes=[
            pltpu.VMEM((4, rows, width), BF16),
            pltpu.VMEM((4, width, 384), BF16),
            pltpu.VMEM((2, 768, 1536), BF16),
            pltpu.VMEM((4, rows, 1536), BF16),
            pltpu.VMEM((2, 96, 1536), BF16),
            pltpu.VMEM((96, 1536), BF16),
            pltpu.VMEM((2, 4, 2, 96, 384), BF16),
            pltpu.VMEM((rows, 768), F32),
            part, part, part, part, part, part,
            pltpu.VMEM((rows, width), F32),
            dma, dma, dma, dma, dma, dma, dma, dma, dma((4,)), dma((4,)), dma((4, 2)), dma((4, 2)),
            dma, dma, dma((4,)), dma((4,)), dma((4, 2)), dma((4, 2)),
            dma((4,)), dma((4,)), dma((4,)), dma((4,)), dma, dma,
            dma((2,)), dma((2,)), dma((2,)), dma((2,)), dma((2,)), dma((2,)),
            dma((4,)), dma((4,)), dma((4,)), dma((4,)),
        ],
        compiler_params=pltpu.CompilerParams(
            collective_id=2, has_side_effects=True, vmem_limit_bytes=56 << 20
        ),
    )(tokens, widen_weight, narrow_weight.T, head_weight.T)


def route_kernel(
    factor, cap, feat, tokpos, counts, rows, head, error, grad,
    buf, mid_x, mid_z, rcv, pred, flags, flags_in, gsum, gpad, pair_in, shares, r1, r2, fin, fin_in,
    s_x, r_x, s_z, r_z, s_xz, r_xz, s_zx, r_zx, s_f, r_f, s_0, r_0, s_1, r_1, s_2, r_2, s_3, r_3,
):
    x, y, z, c = place()
    t, zl = z // 2, lax.rem(z, 2)
    me = 8 * z + 2 * x + c
    owners = 32

    def plane(r):
        nx, nz, nc = lax.rem(x + lax.rem(r // 2, 4), 4), lax.rem(z + r // 8, 4), lax.rem(c + lax.rem(r, 2), 2)
        return device(nx, y, nz, nc), 8 * nz + 2 * nx + nc

    def plane_from(r):
        nx = lax.rem(x + 4 - lax.rem(r // 2, 4), 4)
        nz, nc = lax.rem(z + 4 - r // 8, 4), lax.rem(c + lax.rem(r, 2), 2)
        return device(nx, y, nz, nc), 8 * nz + 2 * nx + nc

    def group(j):
        nt, nd = lax.rem(t + j // 4, 2), lax.rem(y + lax.rem(j, 4), 4)
        return device(x, nd, 2 * nt + zl, c), nt * 4 + nd

    def chip(j):
        nz, nx = lax.rem(zl + j // 4, 2), lax.rem(x + lax.rem(j, 4), 4)
        return device(nx, y, 2 * t + nz, c), 4 * nz + nx

    partner = device(x, y, z, 1 - c)

    barrier = pltpu.get_barrier_semaphore()

    def greet(r, _):
        pl.semaphore_signal(barrier, inc=1, device_id=plane(r)[0], device_id_type=MESH)
        return 0

    lax.fori_loop(1, owners, greet, 0)

    def greet_group(j, _):
        @pl.when(lax.rem(j, 4) != 0)
        def _():
            pl.semaphore_signal(barrier, inc=1, device_id=group(j)[0], device_id_type=MESH)

        return 0

    lax.fori_loop(1, 8, greet_group, 0)

    flags[...] = jnp.broadcast_to(counts[...], (16, 128)).astype(F32).astype(BF16)

    def fill(i, _):
        slot = lax.broadcasted_iota(jnp.int32, (128, feat.shape[0]), 0) + i * 128
        pick = jnp.where(slot == tokpos[...], 1.0, 0.0).astype(BF16)
        block = jnp.dot(pick, feat[...], preferred_element_type=F32).astype(BF16)
        buf[i // 2, pl.ds(2 * lax.rem(i, 2), 2)] = block.reshape(2, 2, 2, 16, -1)
        return 0

    lax.fori_loop(0, owners * cap // 128, fill, 0)

    pl.semaphore_wait(barrier, owners - 1 + 6)

    def along_x(step, core=0):
        nx = lax.rem(x + step, 4)
        return device(nx, y, z, lax.rem(c + core, 2)), nx

    def along_z(step, core=0):
        nz = lax.rem(z + step, 4)
        return device(x, y, nz, lax.rem(c + core, 2)), nz

    for step in (1, 3, 2):
        target, nx = along_x(step)
        send(buf.at[:, nx, :, 0], mid_x.at[x], s_x.at[step], r_x.at[step], target)
        target, nz = along_z(step)
        send(buf.at[nz, :, :, 1], mid_z.at[z], s_z.at[step], r_z.at[step], target)
    mid_x[x] = buf[:, x, :, 0]
    mid_z[z] = buf[z, :, :, 1]

    def out(r, _):
        target, o = plane(r)
        send(flags, flags_in.at[me], s_f.at[o], r_f.at[me], target)
        return 0

    lax.fori_loop(1, owners, out, 0)
    flags_in[me] = flags[...]

    def predict(i, _):
        rows_at = pl.ds(pl.multiple_of(i * 128, 128), 128)
        pred[rows_at, :] = lax.dot_general(
            rows[rows_at, :], head[...], (((1,), (1,)), ((), ())), preferred_element_type=F32
        )
        return 0

    lax.fori_loop(0, owners * cap // 128, predict, 0)
    gsum[...] = jnp.zeros_like(gsum)

    for step in (1, 3, 2):
        wait_recv(mid_x.at[lax.rem(x + 4 - step, 4)], r_x.at[step], partner)
        wait_recv(mid_z.at[lax.rem(z + 4 - step, 4)], r_z.at[step], partner)
    hops = [(step, core) for core in (0, 1) for step in (1, 3, 2, 0) if step + core]
    for step, core in hops:
        nc = lax.rem(c + core, 2)
        at = 2 * step + core
        target, nz = along_z(step, core)
        send(mid_x.at[:, nz, nc], rcv.at[z, :, c, 0], s_xz.at[at], r_xz.at[at], target)
        target, nx = along_x(step, core)
        send(mid_z.at[:, nx, nc], rcv.at[:, x, c, 1], s_zx.at[at], r_zx.at[at], target)
    rcv[z, :, c, 0] = mid_x[:, z, c]
    rcv[:, x, c, 1] = mid_z[:, x, c]

    def flags_from(s, _):
        @pl.when(s != me)
        def _():
            wait_recv(flags_in.at[s], r_f.at[s], partner)

        return 0

    lax.fori_loop(0, owners, flags_from, 0)
    for step, core in hops:
        nc = lax.rem(c + core, 2)
        at = 2 * step + core
        wait_recv(rcv.at[lax.rem(z + 4 - step, 4), :, nc, 0], r_xz.at[at], partner)
        wait_recv(rcv.at[:, lax.rem(x + 4 - step, 4), nc, 1], r_zx.at[at], partner)

    per = 8

    def arrive(i, _):
        rows_at = pl.ds(pl.multiple_of(i * (per * cap), per * cap), per * cap)
        lane = lax.broadcasted_iota(jnp.int32, (per, 16, 128), 2)
        live = flags_in[pl.ds(i * per, per)].astype(F32)
        live = jnp.sum(jnp.where(lane == me, live, 0.0), axis=2, keepdims=True)
        live = jnp.broadcast_to(live[:, None], (per, 2, 16, 1)).reshape(per * cap, 1)
        slot = lax.rem(lax.broadcasted_iota(jnp.int32, (per * cap, 1), 0), cap).astype(F32)
        got = rcv[i].astype(F32).reshape(per * cap, -1)
        wrong = jnp.where(slot < live, pred[rows_at, :] - got, 0.0).astype(BF16)
        error[rows_at, :] = wrong
        gsum[...] += lax.dot_general(
            rows[rows_at, :], wrong, (((0,), (0,)), ((), ())), preferred_element_type=F32
        )
        return 0

    lax.fori_loop(0, 4, arrive, 0)

    wide = gsum.shape[1]
    half = gpad.shape[1] // 2
    gpad[:, :wide] = gsum[...].astype(BF16)
    gpad[:, wide:] = jnp.zeros((gpad.shape[0], 2 * half - wide), BF16)
    theirs = pl.ds(pl.multiple_of((1 - c) * half, half), half)
    ours = pl.ds(pl.multiple_of(c * half, half), half)
    send(gpad.at[:, theirs], pair_in, s_0, r_0, partner)
    wait_recv(pair_in, r_0, partner)
    shares[...] = (gpad[:, ours].astype(F32) + pair_in[...].astype(F32)).astype(BF16)

    block = 48

    def share(j, _):
        target, b = chip(j)
        send(shares.at[pl.ds(pl.multiple_of(b * block, 16), block)], r1.at[j], s_1.at[j], r_1.at[j], target)
        return 0

    lax.fori_loop(1, 8, share, 0)
    own = shares[pl.ds(pl.multiple_of((4 * zl + x) * block, 16), block), :].astype(F32)

    def take(j, total):
        wait_recv(r1.at[j], r_1.at[j], partner)
        return total + r1[j].astype(F32)

    own = lax.fori_loop(1, 8, take, own)
    mine_at = t * 4 + y
    r2[mine_at] = own.astype(BF16)

    def spread(j, _):
        target, b = group(j)
        send(r2.at[mine_at], r2.at[mine_at], s_2.at[b], r_2.at[mine_at], target)
        return 0

    lax.fori_loop(1, 8, spread, 0)

    def settle(b, _):
        @pl.when(b != mine_at)
        def _():
            wait_recv(r2.at[b], r_2.at[b], partner)

        return 0

    lax.fori_loop(0, 8, settle, 0)

    def add(b, total):
        return total + r2[b].astype(F32)

    fin[...] = lax.fori_loop(0, 8, add, jnp.zeros(fin.shape, F32)) * factor
    send(fin, fin_in, s_3, r_3, partner)
    wait_recv(fin_in, r_3, partner)

    @pl.when(c == 0)
    def _():
        grad[:, :half] = fin[:24, :]
        grad[:, half:] = fin_in[:24, : wide - half]

    @pl.when(c == 1)
    def _():
        grad[:, :half] = fin_in[24:, :]
        grad[:, half:] = fin[24:, : wide - half]

    def done(r, _):
        wait_send(flags, s_f.at[plane(r)[1]], partner)
        return 0

    lax.fori_loop(1, owners, done, 0)
    for step in (1, 2, 3):
        wait_send(mid_x.at[x], s_x.at[step], partner)
        wait_send(mid_z.at[z], s_z.at[step], partner)
    for step, core in hops:
        at = 2 * step + core
        wait_send(rcv.at[z, :, c, 0], s_xz.at[at], partner)
        wait_send(rcv.at[:, x, c, 1], s_zx.at[at], partner)

    def done_shares(j, _):
        target, b = chip(j)
        wait_send(shares.at[pl.ds(pl.multiple_of(b * block, 16), block)], s_1.at[j], partner)
        wait_send(r2.at[mine_at], s_2.at[group(j)[1]], partner)
        return 0

    lax.fori_loop(1, 8, done_shares, 0)
    wait_send(gpad.at[:, theirs], s_0, partner)
    wait_send(fin, s_3, partner)


def route(features, tokpos, counts, rows, head, factor, grad_rows):
    slots, width = rows.shape[0], features.shape[1]
    cap = slots // 32
    depth = rows.shape[1]
    half = 768
    dma = pltpu.SemaphoreType.DMA
    vmem = pl.BlockSpec(memory_space=pltpu.VMEM)
    return pl.pallas_call(
        functools.partial(route_kernel, factor, cap),
        out_shape=(
            jax.ShapeDtypeStruct((slots, width), BF16),
            jax.ShapeDtypeStruct((grad_rows, width), F32),
        ),
        in_specs=[vmem] * 5,
        out_specs=(vmem, vmem),
        scratch_shapes=[
            pltpu.VMEM((4, 4, 2, 2, 16, width), BF16),
            pltpu.VMEM((4, 4, 2, 16, width), BF16),
            pltpu.VMEM((4, 4, 2, 16, width), BF16),
            pltpu.VMEM((4, 4, 2, 2, 16, width), BF16),
            pltpu.VMEM((slots, width), F32),
            pltpu.VMEM((16, 128), BF16),
            pltpu.VMEM((32, 16, 128), BF16),
            pltpu.VMEM((depth, width), F32),
            pltpu.VMEM((depth, 2 * half), BF16),
            pltpu.VMEM((depth, half), BF16),
            pltpu.VMEM((depth, half), BF16),
            pltpu.VMEM((8, 48, half), BF16),
            pltpu.VMEM((8, 48, half), BF16),
            pltpu.VMEM((48, half), F32),
            pltpu.VMEM((48, half), F32),
            dma((4,)), dma((4,)), dma((4,)), dma((4,)), dma((8,)), dma((8,)), dma((8,)), dma((8,)),
            dma((32,)), dma((32,)),
            dma, dma, dma((8,)), dma((8,)), dma((8,)), dma((8,)), dma, dma,
        ],
        compiler_params=pltpu.CompilerParams(
            collective_id=1, has_side_effects=True, vmem_limit_bytes=56 << 20
        ),
    )(features, tokpos, counts, rows, head)


def body(
    tokens, widen_weight, narrow_weight, head_weight, predictor_rows, target_index, destination
):
    owners = lax.axis_size("tgt") * lax.axis_size("fsdp")
    devices = owners * lax.axis_size("dp")
    features, head = encode(tokens, widen_weight, narrow_weight, head_weight)
    head = head.reshape(features.shape[1], predictor_rows.shape[1])
    cap = predictor_rows.shape[0] // owners
    routed = destination[:, 0]
    entry = jnp.arange(routed.shape[0], dtype=jnp.int32)
    earlier = (routed[:, None] == routed[None, :]) & (entry[:, None] < entry[None, :])
    position = routed * cap + jnp.sum(earlier.astype(jnp.int32), axis=0)
    token = jnp.arange(tokens.shape[0], dtype=jnp.int32)
    chosen = target_index[:, None] == token[None, :]
    tokpos = jnp.sum(jnp.where(chosen, position[:, None] + 1, 0), axis=0)[None, :] - 1
    lane = jnp.arange(128, dtype=jnp.int32)
    counts = jnp.sum((routed[:, None] == lane[None, :]).astype(jnp.int32), axis=0)[None, :]
    factor = 1.0 / math.sqrt(target_index.shape[0] * devices)
    error, grad = route(
        features, tokpos, counts, predictor_rows, head, factor,
        predictor_rows.shape[1] // lax.axis_size("fsdp"),
    )
    return (features, error, grad)


def solution(mesh):
    in_specs = (
        P(("tgt", "fsdp", "dp"), None),
        P(None, "fsdp"),
        P(None, "fsdp"),
        P(None, "fsdp"),
        P(("tgt", "fsdp", "dp"), None),
        P(("tgt", "fsdp", "dp")),
        P(("tgt", "fsdp", "dp"), None),
    )
    out_specs = (P(("tgt", "fsdp", "dp"), None), P(("tgt", "fsdp", "dp"), None), P("fsdp", None))
    return jax.shard_map(body, mesh=mesh, in_specs=in_specs, out_specs=out_specs, check_vma=False)
```

```python
import functools
import math

import jax
import jax.numpy as jnp
from jax import lax
from jax.experimental import pallas as pl
from jax.experimental.pallas import tpu as pltpu
from jax.sharding import PartitionSpec as P

MESH = pl.DeviceIdType.MESH
F32, BF16 = jnp.float32, jnp.bfloat16


def norm_rows(values):
    center = jnp.mean(values, axis=-1, keepdims=True)
    shifted = values - center
    spread = jnp.mean(shifted * shifted, axis=-1, keepdims=True)
    return shifted * lax.rsqrt(spread + 1e-06)


def place():
    t, f, d = lax.axis_index("tgt"), lax.axis_index("fsdp"), lax.axis_index("dp")
    return lax.rem(f // 2, 4), d, 2 * t + f // 8, lax.rem(f, 2)


def device(x, y, z, c):
    return (z // 2, lax.rem(z, 2) * 8 + x * 2 + c, y)


def send(src, dst, send_sem, recv_sem, target):
    copy = pltpu.make_async_remote_copy(src, dst, send_sem, recv_sem, device_id=target, device_id_type=MESH)
    copy.start()


def wait_recv(dst, sem, target):
    pltpu.make_async_remote_copy(dst, dst, sem, sem, device_id=target, device_id_type=MESH).wait_recv()


def wait_send(src, sem, target):
    pltpu.make_async_remote_copy(src, src, sem, sem, device_id=target, device_id_type=MESH).wait_send()


def gelu(v):
    return 0.5 * v * (1.0 + lax.erf(v * math.sqrt(0.5)))


def kernel(
    factor, cap, tokens, widen, narrow_t, head_t, rows, owner_of, token_of, feats_out, error_out, grad,
    feats, error, xs, w1, w2, hid, nar, nar_in, heads, head, kept, pp_out, pp_in, pc_out, pc_in, py_out, py_in, summed,
    buf_x, buf_z, mid_x, mid_z, rcv, pred, slot_of, flags, flags_in, gpad, pair_in, shares, r1, r2, fin, fin_in,
    s_xp, r_xp, s_xy, r_xy, s_xf, r_xf, s_wp, r_wp, s_wx, r_wx, s_wz, r_wz,
    s_np, r_np, s_nx, r_nx, s_nz, r_nz, s_hx, r_hx, s_hz, r_hz, s_hp, r_hp,
    s_pp, r_pp, s_pc, r_pc, s_py, r_py, s_wf, r_wf, s_nf, r_nf, s_mx, r_mx, s_mf, r_mf,
    s_x, r_x, s_z, r_z, s_xz, r_xz, s_zx, r_zx, s_f, r_f, s_fz, r_fz, s_o, s_0, r_0, s_1, r_1, s_2, r_2, s_3, r_3,
):
    x, y, z, c = place()
    zl, p = lax.rem(z, 2), lax.rem(y, 2)
    partner = device(x, y, z, 1 - c)
    y_up, y_down = lax.rem(y + 1, 4), lax.rem(y + 3, 4)
    z_up = device(x, y, lax.rem(z + 1, 4), c)
    z_down = device(x, y, lax.rem(z + 3, 4), c)
    ahead = lax.select(c == 0, y_up, y_down)
    behind = lax.select(c == 0, y_down, y_up)
    helper, helped = device(x, ahead, z, c), device(x, behind, z, c)
    steps, back = (0, 1, 3, 2), (0, 2, 1, 3)

    def at_x(step):
        return lax.rem(x + step, 4)

    def across(step):
        return device(at_x(step), y, z, c)

    ring = c == zl

    t = z // 2
    me = 8 * z + 2 * x + c
    owners = 32

    def along_x(step, core=0):
        nx = lax.rem(x + step, 4)
        return device(nx, y, z, lax.rem(c + core, 2)), nx

    def along_z(step, core=0):
        nz = lax.rem(z + step, 4)
        return device(x, y, nz, lax.rem(c + core, 2)), nz

    def copy_of(j):
        nt, nd = lax.rem(t + j // 4, 2), lax.rem(y + lax.rem(j, 4), 4)
        return device(x, nd, 2 * nt + zl, c), nt * 4 + nd

    def chip(j):
        nz, nx = lax.rem(zl + j // 4, 2), lax.rem(x + lax.rem(j, 4), 4)
        return device(nx, y, 2 * t + nz, c), 4 * nz + nx


    hops = [(step, core) for core in (0, 1) for step in (1, 3, 2, 0) if step + core]
    barrier = pltpu.get_barrier_semaphore()

    others = [partner]
    others += [along(step, core)[0] for along in (along_x, along_z) for core in (0, 1) for step in (1, 2, 3)]
    others += [chip(j)[0] for j in (5, 6, 7)] + [copy_of(j)[0] for j in (1, 2, 3, 5, 6, 7)]
    for other in others:
        pl.semaphore_signal(barrier, inc=1, device_id=other, device_id_type=MESH)

    xs[0] = norm_rows(tokens[...].astype(F32)).astype(BF16)
    for core in range(2):
        for k in range(4):
            unit = (8 * core + 2 * k + p) * 384
            nar[core, :88, 384 * k : 384 * (k + 1)] = narrow_t[:, pl.ds(pl.multiple_of(unit, 384), 384)]
    nar[:, 88:, :] = jnp.zeros((2, 8, 1536), BF16)
    heads[zl, x, c, :88, :] = head_t[...]
    heads[zl, x, c, 88:, :] = jnp.zeros((8, 384), BF16)
    w2[0, 704:, :] = jnp.zeros((64, 1536), BF16)
    w2[1, :64, :] = jnp.zeros((64, 1536), BF16)
    pl.semaphore_wait(barrier, len(others))

    def spread_z(at):
        send(w1.at[at, pl.ds(0, 704)], w1.at[at, pl.ds(0, 704)], s_wz.at[at, 0], r_wz.at[at, 0], z_up)
        send(w1.at[at, pl.ds(704, 704)], w1.at[at, pl.ds(704, 704)], s_wz.at[at, 1], r_wz.at[at, 1], z_down)

    def spread_x():
        for k in (1, 2):
            send(w1.at[x], w1.at[x], s_wx.at[k], r_wx.at[back[k]], across(steps[k]))

    def pass_x(at, k):
        half = w1.at[at, pl.ds(0, 704)] if k == 2 else w1.at[at, pl.ds(704, 704)]
        send(half, half, s_wf.at[k], r_wf.at[k], across(4 - steps[k]))

    @pl.when((c == p) & (c != zl))
    def _():
        send(widen, w1.at[x], s_wp, r_wp, partner)

    send(nar.at[1 - c], nar_in, s_np, r_np, partner)
    send(xs.at[0], xs.at[2 + c], s_xy, r_xy, helper)

    @pl.when((c == p) & ring)
    def _():
        w1[x] = widen[...]
        spread_x()
        spread_z(x)

    send(xs.at[0], xs.at[1], s_xp, r_xp, partner)

    @pl.when((c != p) & ring)
    def _():
        wait_recv(w1.at[x], r_wp, partner)
        spread_x()
        spread_z(x)

    def hidden(slot, at):
        block = jnp.dot(xs[slot], w1[at], preferred_element_type=F32)
        hid[slot, :, pl.ds(pl.multiple_of(at * 384, 384), 384)] = gelu(block).astype(BF16)

    def all_hidden(at):
        def fill(slot, _):
            hidden(slot, at)
            return 0

        lax.fori_loop(0, 4, fill, 0)

    def piece(side, at):
        return pl.multiple_of(64 * side + 176 * at, 16)

    def upper(side, at):
        return w2.at[side, pl.ds(piece(side, at), 96)]

    def lower(side, at):
        return w2.at[side, pl.ds(pl.multiple_of(piece(side, at) + 96, 16), 80)]

    def part(side, at, first, count):
        return w2.at[side, pl.ds(pl.multiple_of(piece(side, at) + first, 16), count)]

    def spread_narrow_z(at, top, bottom):
        up, down = part(zl, at, 0, top), part(zl, at, 176 - bottom, bottom)
        send(up, up, s_nz.at[at, 0], r_nz.at[at, 0], z_up)
        send(down, down, s_nz.at[at, 1], r_nz.at[at, 1], z_down)

    def narrow_z(at, top, bottom):
        wait_recv(part(1 - zl, at, 0, top), r_nz.at[at, 0], partner)
        wait_recv(part(1 - zl, at, 176 - bottom, bottom), r_nz.at[at, 1], partner)

    def middle_out():
        narrow_z(x, 96, 80)
        rows_mid = part(1 - zl, x, 64, 64)
        for k in (1, 2):
            send(rows_mid, rows_mid, s_mx.at[k], r_mx.at[back[k]], across(steps[k]))

    def middle_pass():
        for k in (1, 2):
            at = at_x(steps[k])
            wait_recv(part(1 - zl, at, 64, 64), r_mx.at[k], partner)
            half = part(1 - zl, at, 64 if k == 2 else 96, 32)
            send(half, half, s_mf.at[k], r_mf.at[k], across(4 - steps[k]))

    def middle_far():
        wait_recv(part(1 - zl, at_x(2), 64, 32), r_mf.at[2], partner)
        wait_recv(part(1 - zl, at_x(2), 96, 32), r_mf.at[1], partner)

    own_cols = w2.at[zl, pl.ds(piece(zl, x), 176)]
    own_head = heads.at[zl, x, c]

    def spread_narrow_x():
        for k in (1, 2):
            send(own_cols, own_cols, s_nx.at[k], r_nx.at[back[k]], across(steps[k]))

    def spread_head_x():
        for k in (1, 2, 3):
            send(own_head, own_head, s_hx.at[k], r_hx.at[back[k]], across(steps[k]))

    def spread_head_z(at):
        src = heads.at[zl, at, c]

        @pl.when(lax.rem(at, 2) == 0)
        def _():
            send(src, src, s_hz.at[at], r_hz.at[at], z_up)

        @pl.when(lax.rem(at, 2) == 1)
        def _():
            send(src, src, s_hz.at[at], r_hz.at[at], z_down)

    def widen_near():
        for k in (1, 2):
            at = at_x(steps[k])
            wait_recv(w1.at[at], r_wx.at[k], partner)
            pass_x(at, k)
            spread_z(at)

    def widen_far():
        at = at_x(2)
        wait_recv(w1.at[at, pl.ds(0, 704)], r_wf.at[2], partner)
        wait_recv(w1.at[at, pl.ds(704, 704)], r_wf.at[1], partner)
        spread_z(at)

    def widen_z(at):
        wait_recv(w1.at[at, pl.ds(0, 704)], r_wz.at[at, 0], partner)
        wait_recv(w1.at[at, pl.ds(704, 704)], r_wz.at[at, 1], partner)

    def narrow_near():
        for k in (1, 2):
            at = at_x(steps[k])
            wait_recv(w2.at[zl, pl.ds(piece(zl, at), 176)], r_nx.at[k], partner)
            half = (upper if k == 2 else lower)(zl, at)
            send(half, half, s_nf.at[k], r_nf.at[k], across(4 - steps[k]))
            spread_narrow_z(at, 64, 48)

    def narrow_far():
        at = at_x(2)
        wait_recv(upper(zl, at), r_nf.at[2], partner)
        wait_recv(lower(zl, at), r_nf.at[1], partner)
        spread_narrow_z(at, 64, 48)

    def indices():
        count = owner_of.shape[1]
        owner = owner_of[...]
        one = jnp.where(lax.broadcasted_iota(jnp.int32, (128, count), 0) == owner, 1.0, 0.0)
        before = lax.broadcasted_iota(jnp.int32, (count, count), 0) < lax.broadcasted_iota(
            jnp.int32, (count, count), 1
        )
        rank = jnp.dot(one.astype(BF16), jnp.where(before, 1.0, 0.0).astype(BF16), preferred_element_type=F32)
        rank = jnp.sum(rank * one, axis=0, keepdims=True)
        flags[...] = lax.dot_general(
            jnp.ones((16, count), BF16), one.astype(BF16), (((1,), (1,)), ((), ())), preferred_element_type=F32
        ).astype(BF16)
        flags_in[z, x, c] = flags[...]
        line = lax.broadcasted_iota(jnp.int32, (8, count), 0)
        known = jnp.where(line == 0, owner.astype(F32) + 1.0, rank).astype(BF16)
        here = lax.broadcasted_iota(jnp.int32, (tokens.shape[0], count), 0) == token_of[...]
        found = lax.dot_general(
            known, jnp.where(here, 1.0, 0.0).astype(BF16), (((1,), (1,)), ((), ())), preferred_element_type=F32
        )
        slot_of[...] = jnp.broadcast_to((found[0:1] - 1.0) * cap + found[1:2], slot_of.shape)

        for step, core in hops:
            at = 2 * step + core
            send(flags, flags_in.at[z, x, c], s_f.at[at], r_f.at[at], along_x(step, core)[0])

    def spread_flags():
        for step, core in hops:
            source = flags_in.at[z, lax.rem(x + 4 - step, 4), lax.rem(c + core, 2)]
            wait_recv(source, r_f.at[2 * step + core], partner)
        for step in (1, 3, 2):
            send(flags_in.at[z], flags_in.at[z], s_fz.at[step], r_fz.at[step], along_z(step)[0])

    def neighbour_rows(at):
        wait_recv(xs.at[2 + c], r_xy, partner)
        send(xs.at[2 + c], xs.at[2 + c], s_xf, r_xf, partner)
        hidden(2 + c, at)
        wait_recv(xs.at[3 - c], r_xf, partner)
        hidden(3 - c, at)

    wait_recv(nar_in, r_np, partner)
    mine, other = nar[c, :88, :].astype(F32), nar_in[:88, :].astype(F32)

    @pl.when(c == 0)
    def _():
        own_cols[...] = jnp.concatenate([mine, other], axis=0).astype(BF16)

    @pl.when(c == 1)
    def _():
        own_cols[...] = jnp.concatenate([other, mine], axis=0).astype(BF16)

    spread_narrow_z(x, 96, 80)

    @pl.when(ring)
    def _():
        hidden(0, x)
        wait_recv(xs.at[1], r_xp, partner)
        hidden(1, x)
        widen_near()
        spread_narrow_x()
        middle_out()
        indices()
        neighbour_rows(x)
        all_hidden(at_x(1))
        widen_far()
        all_hidden(at_x(3))
        narrow_near()
        middle_pass()
        all_hidden(at_x(2))
        narrow_far()

    @pl.when(jnp.logical_not(ring))
    def _():
        spread_narrow_x()
        widen_z(x)
        hidden(0, x)
        wait_recv(xs.at[1], r_xp, partner)
        hidden(1, x)
        narrow_near()
        middle_out()
        indices()
        neighbour_rows(x)
        narrow_far()
        middle_pass()
        for k in (1, 2, 3):
            widen_z(at_x(steps[k]))
            all_hidden(at_x(steps[k]))

    spread_head_x()
    spread_head_z(x)
    spread_flags()

    def partial(slot, side):
        return lax.dot_general(
            hid[slot], w2[side], (((1,), (1,)), ((), ())), preferred_element_type=F32
        )

    def add(value, side):
        @pl.when(side == 0)
        def _():
            summed[:, :768] += value

        @pl.when(side == 1)
        def _():
            summed[:, 640:] += value

    summed[...] = tokens[...].astype(F32)
    for turn in range(2):
        side = zl if turn == 0 else 1 - zl
        if turn == 1:
            middle_far()
            for k in (1, 2, 3):
                narrow_z(at_x(steps[k]), 64, 48)
        pc_out[turn] = partial(3 - c, side).astype(BF16)
        send(pc_out.at[turn], pc_in.at[turn], s_pc.at[turn], r_pc.at[turn], partner)
        kept[...] = partial(2 + c, side)
        wait_recv(pc_in.at[turn], r_pc.at[turn], partner)
        py_out[turn] = (kept[...] + pc_in[turn].astype(F32)).astype(BF16)
        send(py_out.at[turn], py_in.at[turn], s_py.at[turn], r_py.at[turn], helped)
        pp_out[turn] = partial(1, side).astype(BF16)
        send(pp_out.at[turn], pp_in.at[turn], s_pp.at[turn], r_pp.at[turn], partner)
        add(partial(0, side), side)
        if turn == 0:
            for k in (1, 2, 3):
                at = at_x(steps[k])
                wait_recv(heads.at[zl, at, c], r_hx.at[k], partner)
                spread_head_z(at)

    for k in range(4):
        at = at_x(steps[k])
        wait_recv(heads.at[1 - zl, at, c], r_hz.at[at], partner)
    send(heads.at[:, :, c], heads.at[:, :, c], s_hp, r_hp, partner)
    for turn in range(2):
        side = zl if turn == 0 else 1 - zl
        wait_recv(pp_in.at[turn], r_pp.at[turn], partner)
        add(pp_in[turn].astype(F32), side)
        wait_recv(py_in.at[turn], r_py.at[turn], partner)
        add(py_in[turn].astype(F32), side)
    feats[...] = norm_rows(summed[...]).astype(BF16)
    pltpu.make_async_copy(feats, feats_out, s_o.at[4]).start()


    line = lax.broadcasted_iota(jnp.int32, (128, feats.shape[0]), 0)
    outer, inner = line // 32, lax.rem(line // 16, 2) * cap + lax.rem(line, 16)

    def rows_for(slot):
        pick = jnp.where(slot.astype(F32) == slot_of[0:1], 1.0, 0.0).astype(BF16)
        return jnp.dot(pick, feats[...], preferred_element_type=F32).astype(BF16).reshape(4, 2, 16, -1)

    for step in (1, 3, 2):
        target, nx = along_x(step)
        buf_x[nx] = rows_for(outer * (8 * cap) + inner + nx * (2 * cap))
        send(buf_x.at[nx], mid_x.at[x], s_x.at[step], r_x.at[step], target)
        target, nz = along_z(step)
        buf_z[nz] = rows_for(outer * (2 * cap) + inner + nz * (8 * cap) + 16)
        send(buf_z.at[nz], mid_z.at[z], s_z.at[step], r_z.at[step], target)
    mid_x[x] = rows_for(outer * (8 * cap) + inner + x * (2 * cap))
    mid_z[z] = rows_for(outer * (2 * cap) + inner + z * (8 * cap) + 16)

    wait_recv(heads.at[:, :, 1 - c], r_hp, partner)
    for k in range(8):
        both = [heads[k // 4, k % 4, core, :88, :].astype(F32) for core in range(2)]
        head[k] = jnp.concatenate(both, axis=0).astype(BF16)

    def predict(i, _):
        rows_at = pl.ds(pl.multiple_of(i * 128, 128), 128)
        pred[rows_at, :] = lax.dot_general(
            rows[rows_at, :], head[...].reshape(-1, rows.shape[1]), (((1,), (1,)), ((), ())), preferred_element_type=F32
        )
        return 0

    lax.fori_loop(0, owners * cap // 128, predict, 0)
    summed[...] = jnp.zeros_like(summed)

    for step in (1, 3, 2):
        wait_recv(mid_x.at[lax.rem(x + 4 - step, 4)], r_x.at[step], partner)
        wait_recv(mid_z.at[lax.rem(z + 4 - step, 4)], r_z.at[step], partner)
    for step, core in hops:
        nc = lax.rem(c + core, 2)
        at = 2 * step + core
        target, nz = along_z(step, core)
        send(mid_x.at[:, nz, nc], rcv.at[z, :, c, 0], s_xz.at[at], r_xz.at[at], target)
        target, nx = along_x(step, core)
        send(mid_z.at[:, nx, nc], rcv.at[:, x, c, 1], s_zx.at[at], r_zx.at[at], target)
    rcv[z, :, c, 0] = mid_x[:, z, c]
    rcv[:, x, c, 1] = mid_z[:, x, c]

    for step in (1, 3, 2):
        wait_recv(flags_in.at[lax.rem(z + 4 - step, 4)], r_fz.at[step], partner)
    for step, core in hops:
        nc = lax.rem(c + core, 2)
        at = 2 * step + core
        wait_recv(rcv.at[lax.rem(z + 4 - step, 4), :, nc, 0], r_xz.at[at], partner)
        wait_recv(rcv.at[:, lax.rem(x + 4 - step, 4), nc, 1], r_zx.at[at], partner)

    per = 8

    def arrive(i, _):
        rows_at = pl.ds(pl.multiple_of(i * (per * cap), per * cap), per * cap)
        lane = lax.broadcasted_iota(jnp.int32, (per, 16, 128), 2)
        live = flags_in[i].reshape(per, 16, 128).astype(F32)
        live = jnp.sum(jnp.where(lane == me, live, 0.0), axis=2, keepdims=True)
        live = jnp.broadcast_to(live[:, None], (per, 2, 16, 1)).reshape(per * cap, 1)
        slot = lax.rem(lax.broadcasted_iota(jnp.int32, (per * cap, 1), 0), cap).astype(F32)
        got = rcv[i].astype(F32).reshape(per * cap, -1)
        wrong = jnp.where(slot < live, pred[rows_at, :] - got, 0.0).astype(BF16)
        error[rows_at, :] = wrong
        pltpu.make_async_copy(error.at[rows_at], error_out.at[rows_at], s_o.at[i]).start()
        summed[...] += lax.dot_general(
            rows[rows_at, :], wrong, (((0,), (0,)), ((), ())), preferred_element_type=F32
        )
        return 0

    lax.fori_loop(0, 4, arrive, 0)

    wide = summed.shape[1]
    half = gpad.shape[1] // 2
    gpad[:, :wide] = summed[...].astype(BF16)
    gpad[:, wide:] = jnp.zeros((gpad.shape[0], 2 * half - wide), BF16)
    theirs = pl.ds(pl.multiple_of((1 - c) * half, half), half)
    ours = pl.ds(pl.multiple_of(c * half, half), half)
    send(gpad.at[:, theirs], pair_in, s_0, r_0, partner)
    wait_recv(pair_in, r_0, partner)
    shares[...] = (gpad[:, ours].astype(F32) + pair_in[...].astype(F32)).astype(BF16)

    block = 48

    def share(j, _):
        target, b = chip(j)
        send(shares.at[pl.ds(pl.multiple_of(b * block, 16), block)], r1.at[j], s_1.at[j], r_1.at[j], target)
        return 0

    lax.fori_loop(1, 8, share, 0)
    own = shares[pl.ds(pl.multiple_of((4 * zl + x) * block, 16), block), :].astype(F32)

    def take(j, total):
        wait_recv(r1.at[j], r_1.at[j], partner)
        return total + r1[j].astype(F32)

    own = lax.fori_loop(1, 8, take, own)
    mine_at = t * 4 + y
    r2[mine_at] = own.astype(BF16)

    def spread(j, _):
        target, b = copy_of(j)
        send(r2.at[mine_at], r2.at[mine_at], s_2.at[b], r_2.at[mine_at], target)
        return 0

    lax.fori_loop(1, 8, spread, 0)

    def settle(b, _):
        @pl.when(b != mine_at)
        def _():
            wait_recv(r2.at[b], r_2.at[b], partner)

        return 0

    lax.fori_loop(0, 8, settle, 0)

    def add_copy(b, total):
        return total + r2[b].astype(F32)

    fin[...] = lax.fori_loop(0, 8, add_copy, jnp.zeros(fin.shape, F32)) * factor
    send(fin, fin_in, s_3, r_3, partner)
    wait_recv(fin_in, r_3, partner)

    @pl.when(c == 0)
    def _():
        grad[:, :half] = fin[:24, :]
        grad[:, half:] = fin_in[:24, : wide - half]

    @pl.when(c == 1)
    def _():
        grad[:, :half] = fin_in[24:, :]
        grad[:, half:] = fin[24:, : wide - half]

    for step in (1, 2, 3):
        wait_send(flags_in.at[z], s_fz.at[step], partner)
        wait_send(mid_x.at[x], s_x.at[step], partner)
        wait_send(mid_z.at[z], s_z.at[step], partner)
    for step, core in hops:
        at = 2 * step + core
        wait_send(flags, s_f.at[at], partner)
        wait_send(rcv.at[z, :, c, 0], s_xz.at[at], partner)
        wait_send(rcv.at[:, x, c, 1], s_zx.at[at], partner)

    pltpu.make_async_copy(feats, feats_out, s_o.at[4]).wait()
    for i in range(4):
        rows_at = pl.ds(i * per * cap, per * cap)
        pltpu.make_async_copy(error.at[rows_at], error_out.at[rows_at], s_o.at[i]).wait()

    def done_shares(j, _):
        target, b = chip(j)
        wait_send(shares.at[pl.ds(pl.multiple_of(b * block, 16), block)], s_1.at[j], partner)
        wait_send(r2.at[mine_at], s_2.at[copy_of(j)[1]], partner)
        return 0

    lax.fori_loop(1, 8, done_shares, 0)
    wait_send(gpad.at[:, theirs], s_0, partner)
    wait_send(fin, s_3, partner)
    @pl.when((c == p) & (c != zl))
    def _():
        wait_send(widen, s_wp, partner)

    wait_send(xs.at[0], s_xy, partner)
    wait_send(xs.at[0], s_xp, partner)
    wait_send(xs.at[2 + c], s_xf, partner)
    wait_send(nar.at[1 - c], s_np, partner)
    wait_send(heads.at[:, :, c], s_hp, partner)
    for k in range(4):
        at = at_x(steps[k])

        @pl.when(ring)
        def _():
            if k in (1, 2):
                wait_send(w1.at[x], s_wx.at[k], partner)
                wait_send(w1.at[x, pl.ds(0, 704)], s_wf.at[k], partner)
            wait_send(w1.at[at, pl.ds(0, 704)], s_wz.at[at, 0], partner)
            wait_send(w1.at[at, pl.ds(704, 704)], s_wz.at[at, 1], partner)

        if k in (1, 2):
            wait_send(own_cols, s_nx.at[k], partner)
            wait_send((upper if k == 2 else lower)(zl, x), s_nf.at[k], partner)
            wait_send(part(zl, x, 0, 64), s_mx.at[k], partner)
            wait_send(part(zl, x, 0, 32), s_mf.at[k], partner)
        if k:
            wait_send(own_head, s_hx.at[k], partner)
        wait_send(part(zl, at, 0, 64 if k else 96), s_nz.at[at, 0], partner)
        wait_send(part(zl, at, 0, 48 if k else 80), s_nz.at[at, 1], partner)
        wait_send(heads.at[zl, at, c], s_hz.at[at], partner)
    for turn in range(2):
        wait_send(pc_out.at[turn], s_pc.at[turn], partner)
        wait_send(py_out.at[turn], s_py.at[turn], partner)
        wait_send(pp_out.at[turn], s_pp.at[turn], partner)


def step(tokens, widen_weight, narrow_weight, head_weight, predictor_rows, owner_of, token_of, factor):
    count, width = tokens.shape
    slots, depth = predictor_rows.shape
    owners = lax.axis_size("tgt") * lax.axis_size("fsdp")
    cap, half = slots // owners, 768
    dma = pltpu.SemaphoreType.DMA
    vmem = pl.BlockSpec(memory_space=pltpu.VMEM)
    part = pltpu.VMEM((2, count, half), BF16)
    return pl.pallas_call(
        functools.partial(kernel, factor, cap),
        out_shape=(
            jax.ShapeDtypeStruct((count, width), BF16),
            jax.ShapeDtypeStruct((slots, width), BF16),
            jax.ShapeDtypeStruct((depth // lax.axis_size("fsdp"), width), F32),
        ),
        in_specs=[vmem] * 7,
        out_specs=(pl.BlockSpec(memory_space=pl.ANY), pl.BlockSpec(memory_space=pl.ANY), vmem),
        scratch_shapes=[
            pltpu.VMEM((count, width), BF16),
            pltpu.VMEM((slots, width), BF16),
            pltpu.VMEM((4, count, width), BF16),
            pltpu.VMEM((4, width, 384), BF16),
            pltpu.VMEM((2, 768, 1536), BF16),
            pltpu.VMEM((4, count, 1536), BF16),
            pltpu.VMEM((2, 96, 1536), BF16),
            pltpu.VMEM((96, 1536), BF16),
            pltpu.VMEM((2, 4, 2, 96, depth), BF16),
            pltpu.VMEM((8, 176, depth), BF16),
            pltpu.VMEM((count, half), F32),
            part, part, part, part, part, part,
            pltpu.VMEM((count, width), F32),
            pltpu.VMEM((4, 4, 2, 16, width), BF16),
            pltpu.VMEM((4, 4, 2, 16, width), BF16),
            pltpu.VMEM((4, 4, 2, 16, width), BF16),
            pltpu.VMEM((4, 4, 2, 16, width), BF16),
            pltpu.VMEM((4, 4, 2, 2, 16, width), BF16),
            pltpu.VMEM((slots, width), F32),
            pltpu.VMEM((8, count), F32),
            pltpu.VMEM((16, 128), BF16),
            pltpu.VMEM((4, 4, 2, 16, 128), BF16),
            pltpu.VMEM((depth, 2 * half), BF16),
            pltpu.VMEM((depth, half), BF16),
            pltpu.VMEM((depth, half), BF16),
            pltpu.VMEM((8, 48, half), BF16),
            pltpu.VMEM((8, 48, half), BF16),
            pltpu.VMEM((48, half), F32),
            pltpu.VMEM((48, half), F32),
            dma, dma, dma, dma, dma, dma, dma, dma, dma((4,)), dma((4,)), dma((4, 2)), dma((4, 2)),
            dma, dma, dma((4,)), dma((4,)), dma((4, 2)), dma((4, 2)),
            dma((4,)), dma((4,)), dma((4,)), dma((4,)), dma, dma,
            dma((2,)), dma((2,)), dma((2,)), dma((2,)), dma((2,)), dma((2,)),
            dma((4,)), dma((4,)), dma((4,)), dma((4,)), dma((4,)), dma((4,)), dma((4,)), dma((4,)),
            dma((4,)), dma((4,)), dma((4,)), dma((4,)), dma((8,)), dma((8,)), dma((8,)), dma((8,)),
            dma((8,)), dma((8,)), dma((4,)), dma((4,)), dma((5,)),
            dma, dma, dma((8,)), dma((8,)), dma((8,)), dma((8,)), dma, dma,
        ],
        compiler_params=pltpu.CompilerParams(
            collective_id=1, has_side_effects=True, vmem_limit_bytes=62 << 20
        ),
    )(
        tokens, widen_weight, narrow_weight.T, head_weight.T, predictor_rows, owner_of, token_of
    )


def body(
    tokens, widen_weight, narrow_weight, head_weight, predictor_rows, target_index, destination
):
    devices = lax.axis_size("tgt") * lax.axis_size("fsdp") * lax.axis_size("dp")
    entries = target_index.shape[0]
    return step(
        tokens, widen_weight, narrow_weight, head_weight, predictor_rows,
        destination.reshape(1, entries), target_index.reshape(1, entries),
        1.0 / math.sqrt(entries * devices),
    )


def solution(mesh):
    in_specs = (
        P(("tgt", "fsdp", "dp"), None),
        P(None, "fsdp"),
        P(None, "fsdp"),
        P(None, "fsdp"),
        P(("tgt", "fsdp", "dp"), None),
        P(("tgt", "fsdp", "dp")),
        P(("tgt", "fsdp", "dp"), None),
    )
    out_specs = (P(("tgt", "fsdp", "dp"), None), P(("tgt", "fsdp", "dp"), None), P("fsdp", None))
    return jax.shard_map(body, mesh=mesh, in_specs=in_specs, out_specs=out_specs, check_vma=False)
```

```python
import functools
import math

import jax
import jax.numpy as jnp
from jax import lax
from jax.experimental import pallas as pl
from jax.experimental.pallas import tpu as pltpu
from jax.sharding import PartitionSpec as P

MESH = pl.DeviceIdType.MESH
F32, BF16 = jnp.float32, jnp.bfloat16


def norm_rows(values):
    center = jnp.mean(values, axis=-1, keepdims=True)
    shifted = values - center
    spread = jnp.mean(shifted * shifted, axis=-1, keepdims=True)
    return shifted * lax.rsqrt(spread + 1e-06)


def place():
    t, f, d = lax.axis_index("tgt"), lax.axis_index("fsdp"), lax.axis_index("dp")
    return lax.rem(f // 2, 4), d, 2 * t + f // 8, lax.rem(f, 2)


def device(x, y, z, c):
    return (z // 2, lax.rem(z, 2) * 8 + x * 2 + c, y)


def send(src, dst, send_sem, recv_sem, target):
    copy = pltpu.make_async_remote_copy(src, dst, send_sem, recv_sem, device_id=target, device_id_type=MESH)
    copy.start()


def wait_recv(dst, sem, target):
    pltpu.make_async_remote_copy(dst, dst, sem, sem, device_id=target, device_id_type=MESH).wait_recv()


def wait_send(src, sem, target):
    pltpu.make_async_remote_copy(src, src, sem, sem, device_id=target, device_id_type=MESH).wait_send()


def gelu(v):
    return 0.5 * v * (1.0 + lax.erf(v * math.sqrt(0.5)))


def kernel(
    factor, cap, tokens, widen, narrow_t, head_t, rows, owner_of, token_of, feats_out, error_out, grad,
    feats, error, xs, w1, w2, hid, nar, nar_in, heads, head, kept, pp_out, pp_in, pc_out, pc_in, py_out, py_in, summed,
    buf_x, buf_z, mid_x, mid_z, rcv, pred, slot_of, flags, flags_in, pair_out, pair_in, shares, r1, r_own, r2, fin, gout,
    s_xp, r_xp, s_xy, r_xy, s_xf, r_xf, s_wp, r_wp, s_wx, r_wx, s_wz, r_wz,
    s_np, r_np, s_nx, r_nx, s_nz, r_nz, s_hx, r_hx, s_hz, r_hz, s_hp, r_hp,
    s_pp, r_pp, s_pc, r_pc, s_py, r_py, s_wf, r_wf, s_nf, r_nf, s_mx, r_mx, s_mf, r_mf,
    s_x, r_x, s_z, r_z, s_xz, r_xz, s_zx, r_zx, s_f, r_f, s_fz, r_fz, s_o, s_0, r_0, s_1, r_1, s_2, r_2, s_3, r_3,
):
    x, y, z, c = place()
    zl, p = lax.rem(z, 2), lax.rem(y, 2)
    partner = device(x, y, z, 1 - c)
    y_up, y_down = lax.rem(y + 1, 4), lax.rem(y + 3, 4)
    z_up = device(x, y, lax.rem(z + 1, 4), c)
    z_down = device(x, y, lax.rem(z + 3, 4), c)
    ahead = lax.select(c == 0, y_up, y_down)
    behind = lax.select(c == 0, y_down, y_up)
    helper, helped = device(x, ahead, z, c), device(x, behind, z, c)
    steps, back = (0, 1, 3, 2), (0, 2, 1, 3)

    def at_x(step):
        return lax.rem(x + step, 4)

    def across(step):
        return device(at_x(step), y, z, c)

    ring = c == zl

    t = z // 2
    me = 8 * z + 2 * x + c
    owners = 32

    def along_x(step, core=0):
        nx = lax.rem(x + step, 4)
        return device(nx, y, z, lax.rem(c + core, 2)), nx

    def along_z(step, core=0):
        nz = lax.rem(z + step, 4)
        return device(x, y, nz, lax.rem(c + core, 2)), nz

    def copy_of(j):
        nt, nd = lax.rem(t + j // 4, 2), lax.rem(y + lax.rem(j, 4), 4)
        return device(x, nd, 2 * nt + zl, c), nt * 4 + nd

    def chip(j):
        nz, nx = lax.rem(zl + j // 4, 2), lax.rem(x + lax.rem(j, 4), 4)
        return device(nx, y, 2 * t + nz, c), 4 * nz + nx


    hops = [(step, core) for core in (0, 1) for step in (1, 3, 2, 0) if step + core]
    barrier = pltpu.get_barrier_semaphore()

    others = [partner]
    others += [along(step, core)[0] for along in (along_x, along_z) for core in (0, 1) for step in (1, 2, 3)]
    others += [chip(j)[0] for j in (5, 6, 7)] + [copy_of(j)[0] for j in (1, 2, 3, 5, 6, 7)]
    others += [device(x, lax.rem(y + dy, 4), lax.rem(z + dz, 4), 1 - c) for dz in (0, 2) for dy in (1, 2, 3)]
    for other in others:
        pl.semaphore_signal(barrier, inc=1, device_id=other, device_id_type=MESH)

    xs[0] = norm_rows(tokens[...].astype(F32)).astype(BF16)
    for core in range(2):
        for k in range(4):
            unit = (8 * core + 2 * k + p) * 384
            nar[core, :88, 384 * k : 384 * (k + 1)] = narrow_t[:, pl.ds(pl.multiple_of(unit, 384), 384)]
    nar[:, 88:, :] = jnp.zeros((2, 8, 1536), BF16)
    heads[zl, x, c, :88, :] = head_t[...]
    heads[zl, x, c, 88:, :] = jnp.zeros((8, 384), BF16)
    w2[0, 704:, :] = jnp.zeros((64, 1536), BF16)
    w2[1, :64, :] = jnp.zeros((64, 1536), BF16)
    pl.semaphore_wait(barrier, len(others))

    def spread_z(at):
        send(w1.at[at, pl.ds(0, 704)], w1.at[at, pl.ds(0, 704)], s_wz.at[at, 0], r_wz.at[at, 0], z_up)
        send(w1.at[at, pl.ds(704, 704)], w1.at[at, pl.ds(704, 704)], s_wz.at[at, 1], r_wz.at[at, 1], z_down)

    def spread_x():
        for k in (1, 2):
            send(w1.at[x], w1.at[x], s_wx.at[k - 1], r_wx.at[back[k] - 1], across(steps[k]))

    def pass_x(at, k):
        half = w1.at[at, pl.ds(0, 704)] if k == 2 else w1.at[at, pl.ds(704, 704)]
        send(half, half, s_wf.at[k - 1], r_wf.at[k - 1], across(4 - steps[k]))

    @pl.when((c == p) & (c != zl))
    def _():
        send(widen, w1.at[x], s_wp, r_wp, partner)

    send(nar.at[1 - c], nar_in, s_np, r_np, partner)
    send(xs.at[0], xs.at[2 + c], s_xy, r_xy, helper)

    @pl.when((c == p) & ring)
    def _():
        w1[x] = widen[...]
        spread_x()
        spread_z(x)

    send(xs.at[0], xs.at[1], s_xp, r_xp, partner)

    @pl.when((c != p) & ring)
    def _():
        wait_recv(w1.at[x], r_wp, partner)
        spread_x()
        spread_z(x)

    def hidden(slot, at):
        block = jnp.dot(xs[slot], w1[at], preferred_element_type=F32)
        hid[slot, :, pl.ds(pl.multiple_of(at * 384, 384), 384)] = gelu(block).astype(BF16)

    def all_hidden(at):
        def fill(slot, _):
            hidden(slot, at)
            return 0

        lax.fori_loop(0, 4, fill, 0)

    def half_hidden(first, at):
        hidden(first, at)
        hidden(first + 1, at)

    def piece(side, at):
        return pl.multiple_of(64 * side + 176 * at, 16)

    def upper(side, at):
        return w2.at[side, pl.ds(piece(side, at), 96)]

    def lower(side, at):
        return w2.at[side, pl.ds(pl.multiple_of(piece(side, at) + 96, 16), 80)]

    def part(side, at, first, count):
        return w2.at[side, pl.ds(pl.multiple_of(piece(side, at) + first, 16), count)]

    def spread_narrow_z(at, top, bottom):
        up, down = part(zl, at, 0, top), part(zl, at, 176 - bottom, bottom)
        send(up, up, s_nz.at[at, 0], r_nz.at[at, 0], z_up)
        send(down, down, s_nz.at[at, 1], r_nz.at[at, 1], z_down)

    def narrow_z(at, top, bottom):
        wait_recv(part(1 - zl, at, 0, top), r_nz.at[at, 0], partner)
        wait_recv(part(1 - zl, at, 176 - bottom, bottom), r_nz.at[at, 1], partner)

    def middle_out():
        narrow_z(x, 96, 80)
        rows_mid = part(1 - zl, x, 64, 64)
        for k in (1, 2):
            send(rows_mid, rows_mid, s_mx.at[k - 1], r_mx.at[back[k] - 1], across(steps[k]))

    def middle_pass():
        for k in (1, 2):
            at = at_x(steps[k])
            wait_recv(part(1 - zl, at, 64, 64), r_mx.at[k - 1], partner)
            half = part(1 - zl, at, 64 if k == 2 else 96, 32)
            send(half, half, s_mf.at[k - 1], r_mf.at[k - 1], across(4 - steps[k]))

    def middle_far():
        wait_recv(part(1 - zl, at_x(2), 64, 32), r_mf.at[1], partner)
        wait_recv(part(1 - zl, at_x(2), 96, 32), r_mf.at[0], partner)

    own_cols = w2.at[zl, pl.ds(piece(zl, x), 176)]
    own_head = heads.at[zl, x, c]

    def spread_narrow_x():
        for k in (1, 2):
            send(own_cols, own_cols, s_nx.at[k - 1], r_nx.at[back[k] - 1], across(steps[k]))

    def spread_head_x():
        for k in (1, 2, 3):
            send(own_head, own_head, s_hx.at[k], r_hx.at[back[k]], across(steps[k]))

    def spread_head_z(at):
        src = heads.at[zl, at, c]

        @pl.when(lax.rem(at, 2) == 0)
        def _():
            send(src, src, s_hz.at[at], r_hz.at[at], z_up)

        @pl.when(lax.rem(at, 2) == 1)
        def _():
            send(src, src, s_hz.at[at], r_hz.at[at], z_down)

    def widen_near():
        for k in (1, 2):
            at = at_x(steps[k])
            wait_recv(w1.at[at], r_wx.at[k - 1], partner)
            pass_x(at, k)
            spread_z(at)

    def widen_far():
        at = at_x(2)
        wait_recv(w1.at[at, pl.ds(0, 704)], r_wf.at[1], partner)
        wait_recv(w1.at[at, pl.ds(704, 704)], r_wf.at[0], partner)
        spread_z(at)

    def widen_z(at):
        wait_recv(w1.at[at, pl.ds(0, 704)], r_wz.at[at, 0], partner)
        wait_recv(w1.at[at, pl.ds(704, 704)], r_wz.at[at, 1], partner)

    def narrow_near():
        for k in (1, 2):
            at = at_x(steps[k])
            wait_recv(w2.at[zl, pl.ds(piece(zl, at), 176)], r_nx.at[k - 1], partner)
            half = (upper if k == 2 else lower)(zl, at)
            send(half, half, s_nf.at[k - 1], r_nf.at[k - 1], across(4 - steps[k]))
            spread_narrow_z(at, 64, 48)

    def narrow_far():
        at = at_x(2)
        wait_recv(upper(zl, at), r_nf.at[1], partner)
        wait_recv(lower(zl, at), r_nf.at[0], partner)
        spread_narrow_z(at, 64, 48)

    def indices():
        count = owner_of.shape[1]
        owner = owner_of[...]
        one = jnp.where(lax.broadcasted_iota(jnp.int32, (128, count), 0) == owner, 1.0, 0.0)
        before = lax.broadcasted_iota(jnp.int32, (count, count), 0) < lax.broadcasted_iota(
            jnp.int32, (count, count), 1
        )
        rank = jnp.dot(one.astype(BF16), jnp.where(before, 1.0, 0.0).astype(BF16), preferred_element_type=F32)
        rank = jnp.sum(rank * one, axis=0, keepdims=True)
        flags[...] = lax.dot_general(
            jnp.ones((16, count), BF16), one.astype(BF16), (((1,), (1,)), ((), ())), preferred_element_type=F32
        ).astype(BF16)
        flags_in[z, x, c] = flags[...]
        line = lax.broadcasted_iota(jnp.int32, (8, count), 0)
        known = jnp.where(line == 0, owner.astype(F32) + 1.0, rank).astype(BF16)
        here = lax.broadcasted_iota(jnp.int32, (tokens.shape[0], count), 0) == token_of[...]
        found = lax.dot_general(
            known, jnp.where(here, 1.0, 0.0).astype(BF16), (((1,), (1,)), ((), ())), preferred_element_type=F32
        )
        slot_of[...] = jnp.broadcast_to((found[0:1] - 1.0) * cap + found[1:2], slot_of.shape)

        for step, core in hops:
            at = 2 * step + core
            send(flags, flags_in.at[z, x, c], s_f.at[at], r_f.at[at], along_x(step, core)[0])

    def spread_flags():
        for step, core in hops:
            source = flags_in.at[z, lax.rem(x + 4 - step, 4), lax.rem(c + core, 2)]
            wait_recv(source, r_f.at[2 * step + core], partner)
        for step in (1, 3, 2):
            send(flags_in.at[z], flags_in.at[z], s_fz.at[step], r_fz.at[step], along_z(step)[0])

    def neighbour_rows(at):
        wait_recv(xs.at[2 + c], r_xy, partner)
        send(xs.at[2 + c], xs.at[2 + c], s_xf, r_xf, partner)
        hidden(2 + c, at)
        wait_recv(xs.at[3 - c], r_xf, partner)
        hidden(3 - c, at)

    wait_recv(nar_in, r_np, partner)
    mine, other = nar[c, :88, :].astype(F32), nar_in[:88, :].astype(F32)

    @pl.when(c == 0)
    def _():
        own_cols[...] = jnp.concatenate([mine, other], axis=0).astype(BF16)

    @pl.when(c == 1)
    def _():
        own_cols[...] = jnp.concatenate([other, mine], axis=0).astype(BF16)

    spread_narrow_z(x, 96, 80)

    @pl.when(ring)
    def _():
        hidden(0, x)
        wait_recv(xs.at[1], r_xp, partner)
        hidden(1, x)
        widen_near()
        spread_narrow_x()
        middle_out()
        indices()
        neighbour_rows(x)
        half_hidden(0, at_x(1))
        widen_far()
        half_hidden(2, at_x(1))
        narrow_near()
        half_hidden(0, at_x(3))
        middle_pass()
        half_hidden(2, at_x(3))
        narrow_far()
        all_hidden(at_x(2))

    @pl.when(jnp.logical_not(ring))
    def _():
        spread_narrow_x()
        widen_z(x)
        hidden(0, x)
        wait_recv(xs.at[1], r_xp, partner)
        hidden(1, x)
        narrow_near()
        middle_out()
        indices()
        neighbour_rows(x)
        narrow_far()
        middle_pass()
        for k in (1, 2, 3):
            widen_z(at_x(steps[k]))
            all_hidden(at_x(steps[k]))

    spread_head_x()
    spread_head_z(x)
    spread_flags()

    def partial(slot, side):
        return lax.dot_general(
            hid[slot], w2[side], (((1,), (1,)), ((), ())), preferred_element_type=F32
        )

    def add(value, side):
        @pl.when(side == 0)
        def _():
            summed[:, :768] += value

        @pl.when(side == 1)
        def _():
            summed[:, 640:] += value

    summed[...] = tokens[...].astype(F32)
    for turn in range(2):
        side = zl if turn == 0 else 1 - zl
        if turn == 1:
            middle_far()
            for k in (1, 2, 3):
                narrow_z(at_x(steps[k]), 64, 48)
        pc_out[turn] = partial(3 - c, side).astype(BF16)
        send(pc_out.at[turn], pc_in.at[turn], s_pc.at[turn], r_pc.at[turn], partner)
        kept[...] = partial(2 + c, side)
        wait_recv(pc_in.at[turn], r_pc.at[turn], partner)
        py_out[turn] = (kept[...] + pc_in[turn].astype(F32)).astype(BF16)
        send(py_out.at[turn], py_in.at[turn], s_py.at[turn], r_py.at[turn], helped)
        pp_out[turn] = partial(1, side).astype(BF16)
        send(pp_out.at[turn], pp_in.at[turn], s_pp.at[turn], r_pp.at[turn], partner)
        add(partial(0, side), side)
        if turn == 0:
            for k in (1, 2, 3):
                at = at_x(steps[k])
                wait_recv(heads.at[zl, at, c], r_hx.at[k], partner)
                spread_head_z(at)

    for k in range(4):
        at = at_x(steps[k])
        wait_recv(heads.at[1 - zl, at, c], r_hz.at[at], partner)
    send(heads.at[:, :, c], heads.at[:, :, c], s_hp, r_hp, partner)
    for turn in range(2):
        side = zl if turn == 0 else 1 - zl
        wait_recv(pp_in.at[turn], r_pp.at[turn], partner)
        add(pp_in[turn].astype(F32), side)
        wait_recv(py_in.at[turn], r_py.at[turn], partner)
        add(py_in[turn].astype(F32), side)
    feats[...] = norm_rows(summed[...]).astype(BF16)
    pltpu.make_async_copy(feats, feats_out, s_o.at[4]).start()


    line = lax.broadcasted_iota(jnp.int32, (128, feats.shape[0]), 0)
    outer, inner = line // 32, lax.rem(line // 16, 2) * cap + lax.rem(line, 16)

    def rows_for(slot):
        pick = jnp.where(slot.astype(F32) == slot_of[0:1], 1.0, 0.0).astype(BF16)
        return jnp.dot(pick, feats[...], preferred_element_type=F32).astype(BF16).reshape(4, 2, 16, -1)

    for step in (1, 3, 2):
        target, nx = along_x(step)
        buf_x[nx] = rows_for(outer * (8 * cap) + inner + nx * (2 * cap))
        send(buf_x.at[nx], mid_x.at[x], s_x.at[step], r_x.at[step], target)
        target, nz = along_z(step)
        buf_z[nz] = rows_for(outer * (2 * cap) + inner + nz * (8 * cap) + 16)
        send(buf_z.at[nz], mid_z.at[z], s_z.at[step], r_z.at[step], target)
    mid_x[x] = rows_for(outer * (8 * cap) + inner + x * (2 * cap))
    mid_z[z] = rows_for(outer * (2 * cap) + inner + z * (8 * cap) + 16)

    wait_recv(heads.at[:, :, 1 - c], r_hp, partner)
    for k in range(8):
        both = [heads[k // 4, k % 4, core, :88, :].astype(F32) for core in range(2)]
        head[k] = jnp.concatenate(both, axis=0).astype(BF16)

    def predict(i, _):
        rows_at = pl.ds(pl.multiple_of(i * 128, 128), 128)
        pred[rows_at, :] = lax.dot_general(
            rows[rows_at, :], head[...].reshape(-1, rows.shape[1]), (((1,), (1,)), ((), ())), preferred_element_type=F32
        )
        return 0

    lax.fori_loop(0, owners * cap // 128, predict, 0)
    width, half = feats.shape[1], pair_in.shape[1]
    error[:, width:] = jnp.zeros((error.shape[0], 2 * half - width), BF16)

    for step in (1, 3, 2):
        wait_recv(mid_x.at[lax.rem(x + 4 - step, 4)], r_x.at[step], partner)
        wait_recv(mid_z.at[lax.rem(z + 4 - step, 4)], r_z.at[step], partner)
    for step, core in hops:
        nc = lax.rem(c + core, 2)
        at = 2 * step + core
        target, nz = along_z(step, core)
        send(mid_x.at[:, nz, nc], rcv.at[z, :, c, 0], s_xz.at[at], r_xz.at[at], target)
        target, nx = along_x(step, core)
        send(mid_z.at[:, nx, nc], rcv.at[:, x, c, 1], s_zx.at[at], r_zx.at[at], target)
    rcv[z, :, c, 0] = mid_x[:, z, c]
    rcv[:, x, c, 1] = mid_z[:, x, c]

    for step in (1, 3, 2):
        wait_recv(flags_in.at[lax.rem(z + 4 - step, 4)], r_fz.at[step], partner)
    for step, core in hops:
        nc = lax.rem(c + core, 2)
        at = 2 * step + core
        wait_recv(rcv.at[lax.rem(z + 4 - step, 4), :, nc, 0], r_xz.at[at], partner)
        wait_recv(rcv.at[:, lax.rem(x + 4 - step, 4), nc, 1], r_zx.at[at], partner)

    per = 8

    def arrive(i, _):
        rows_at = pl.ds(pl.multiple_of(i * (per * cap), per * cap), per * cap)
        lane = lax.broadcasted_iota(jnp.int32, (per, 16, 128), 2)
        live = flags_in[i].reshape(per, 16, 128).astype(F32)
        live = jnp.sum(jnp.where(lane == me, live, 0.0), axis=2, keepdims=True)
        live = jnp.broadcast_to(live[:, None], (per, 2, 16, 1)).reshape(per * cap, 1)
        slot = lax.rem(lax.broadcasted_iota(jnp.int32, (per * cap, 1), 0), cap).astype(F32)
        got = rcv[i].astype(F32).reshape(per * cap, -1)
        wrong = jnp.where(slot < live, pred[rows_at, :] - got, 0.0).astype(BF16)
        error[rows_at, :width] = wrong
        pltpu.make_async_copy(error.at[rows_at, pl.ds(0, width)], error_out.at[rows_at], s_o.at[i]).start()
        return 0

    lax.fori_loop(0, 4, arrive, 0)

    def product(core):
        columns = error[:, pl.ds(pl.multiple_of(core * half, half), half)]
        return lax.dot_general(
            rows[...], columns, (((0,), (0,)), ((), ())), preferred_element_type=F32
        )

    pair_out[...] = product(1 - c).astype(BF16)
    send(pair_out, pair_in, s_0, r_0, partner)
    kept[...] = product(c)
    wait_recv(pair_in, r_0, partner)
    shares[...] = (kept[...] + pair_in[...].astype(F32)).astype(BF16)

    block = 48

    def share(j, _):
        target, b = chip(j)
        send(shares.at[pl.ds(pl.multiple_of(b * block, 16), block)], r1.at[j], s_1.at[j], r_1.at[j], target)
        return 0

    lax.fori_loop(1, 8, share, 0)
    own = shares[pl.ds(pl.multiple_of((4 * zl + x) * block, 16), block), :].astype(F32)

    def take(j, total):
        wait_recv(r1.at[j], r_1.at[j], partner)
        return total + r1[j].astype(F32)

    own = lax.fori_loop(1, 8, take, own)
    mine_at = t * 4 + y
    r_own[...] = own.astype(BF16)

    def holder(r, core):
        return device(x, lax.rem(r, 4), 2 * (r // 4) + zl, core)

    def columns_of(r):
        return pl.ds(pl.multiple_of(r * 128, 128), 128)

    def scatter(r, _):
        @pl.when(r != mine_at)
        def _():
            send(r_own.at[:, columns_of(r)], r2.at[mine_at], s_2.at[r], r_2.at[mine_at], holder(r, c))

        return 0

    lax.fori_loop(0, 6 - c, scatter, 0)
    made = 6 * c + mine_at

    @pl.when(mine_at < 6 - c)
    def _():
        r2[mine_at] = r_own[:, columns_of(mine_at)]

        def settle(r, _):
            @pl.when(r != mine_at)
            def _():
                wait_recv(r2.at[r], r_2.at[r], partner)

            return 0

        lax.fori_loop(0, 8, settle, 0)
        total = r2[0].astype(F32)
        for r in range(1, 8):
            total = total + r2[r].astype(F32)
        fin[...] = (total * factor).reshape(2, 24, 128)

        def hand_out(q, _):
            r, core = q // 2, lax.rem(q, 2)

            @pl.when((r != mine_at) | (core != c))
            def _():
                send(fin.at[core], gout.at[:, columns_of(made)], s_3.at[q], r_3.at[made], holder(r, core))

            return 0

        lax.fori_loop(0, 16, hand_out, 0)
        gout[:, columns_of(made)] = fin[c]

    def collect(i, _):
        @pl.when((i != made) | (mine_at >= 6 - c))
        def _():
            wait_recv(gout.at[:, columns_of(i)], r_3.at[i], partner)

        return 0

    lax.fori_loop(0, 11, collect, 0)
    grad[...] = gout[...]

    for step in (1, 2, 3):
        wait_send(flags_in.at[z], s_fz.at[step], partner)
        wait_send(mid_x.at[x], s_x.at[step], partner)
        wait_send(mid_z.at[z], s_z.at[step], partner)
    for step, core in hops:
        at = 2 * step + core
        wait_send(flags, s_f.at[at], partner)
        wait_send(rcv.at[z, :, c, 0], s_xz.at[at], partner)
        wait_send(rcv.at[:, x, c, 1], s_zx.at[at], partner)
    pltpu.make_async_copy(feats, feats_out, s_o.at[4]).wait()
    for i in range(4):
        rows_at = pl.ds(i * per * cap, per * cap)
        pltpu.make_async_copy(error.at[rows_at, pl.ds(0, width)], error_out.at[rows_at], s_o.at[i]).wait()

    def done_shares(j, _):
        target, b = chip(j)
        wait_send(shares.at[pl.ds(pl.multiple_of(b * block, 16), block)], s_1.at[j], partner)
        return 0

    lax.fori_loop(1, 8, done_shares, 0)

    def done_scatter(r, _):
        @pl.when(r != mine_at)
        def _():
            wait_send(r_own.at[:, columns_of(r)], s_2.at[r], partner)

        return 0

    lax.fori_loop(0, 6 - c, done_scatter, 0)

    @pl.when(mine_at < 6 - c)
    def _():
        def handed(q, _):
            @pl.when((q // 2 != mine_at) | (lax.rem(q, 2) != c))
            def _():
                wait_send(fin.at[0], s_3.at[q], partner)

            return 0

        lax.fori_loop(0, 16, handed, 0)

    wait_send(pair_out, s_0, partner)
    @pl.when((c == p) & (c != zl))
    def _():
        wait_send(widen, s_wp, partner)

    wait_send(xs.at[0], s_xy, partner)
    wait_send(xs.at[0], s_xp, partner)
    wait_send(xs.at[2 + c], s_xf, partner)
    wait_send(nar.at[1 - c], s_np, partner)
    wait_send(heads.at[:, :, c], s_hp, partner)
    for k in range(4):
        at = at_x(steps[k])

        @pl.when(ring)
        def _():
            if k in (1, 2):
                wait_send(w1.at[x], s_wx.at[k - 1], partner)
                wait_send(w1.at[x, pl.ds(0, 704)], s_wf.at[k - 1], partner)
            wait_send(w1.at[at, pl.ds(0, 704)], s_wz.at[at, 0], partner)
            wait_send(w1.at[at, pl.ds(704, 704)], s_wz.at[at, 1], partner)

        if k in (1, 2):
            wait_send(own_cols, s_nx.at[k - 1], partner)
            wait_send((upper if k == 2 else lower)(zl, x), s_nf.at[k - 1], partner)
            wait_send(part(zl, x, 0, 64), s_mx.at[k - 1], partner)
            wait_send(part(zl, x, 0, 32), s_mf.at[k - 1], partner)
        if k:
            wait_send(own_head, s_hx.at[k], partner)
        wait_send(part(zl, at, 0, 64 if k else 96), s_nz.at[at, 0], partner)
        wait_send(part(zl, at, 0, 48 if k else 80), s_nz.at[at, 1], partner)
        wait_send(heads.at[zl, at, c], s_hz.at[at], partner)
    for turn in range(2):
        wait_send(pc_out.at[turn], s_pc.at[turn], partner)
        wait_send(py_out.at[turn], s_py.at[turn], partner)
        wait_send(pp_out.at[turn], s_pp.at[turn], partner)


def step(tokens, widen_weight, narrow_weight, head_weight, predictor_rows, owner_of, token_of, factor):
    count, width = tokens.shape
    slots, depth = predictor_rows.shape
    owners = lax.axis_size("tgt") * lax.axis_size("fsdp")
    cap, half = slots // owners, 768
    dma = pltpu.SemaphoreType.DMA
    vmem = pl.BlockSpec(memory_space=pltpu.VMEM)
    part = pltpu.VMEM((2, count, half), BF16)
    return pl.pallas_call(
        functools.partial(kernel, factor, cap),
        out_shape=(
            jax.ShapeDtypeStruct((count, width), BF16),
            jax.ShapeDtypeStruct((slots, width), BF16),
            jax.ShapeDtypeStruct((depth // lax.axis_size("fsdp"), width), F32),
        ),
        in_specs=[vmem] * 7,
        out_specs=(pl.BlockSpec(memory_space=pl.ANY), pl.BlockSpec(memory_space=pl.ANY), vmem),
        scratch_shapes=[
            pltpu.VMEM((count, width), BF16),
            pltpu.VMEM((slots, 2 * half), BF16),
            pltpu.VMEM((4, count, width), BF16),
            pltpu.VMEM((4, width, 384), BF16),
            pltpu.VMEM((2, 768, 1536), BF16),
            pltpu.VMEM((4, count, 1536), BF16),
            pltpu.VMEM((2, 96, 1536), BF16),
            pltpu.VMEM((96, 1536), BF16),
            pltpu.VMEM((2, 4, 2, 96, depth), BF16),
            pltpu.VMEM((8, 176, depth), BF16),
            pltpu.VMEM((count, half), F32),
            part, part, part, part, part, part,
            pltpu.VMEM((count, width), F32),
            pltpu.VMEM((4, 4, 2, 16, width), BF16),
            pltpu.VMEM((4, 4, 2, 16, width), BF16),
            pltpu.VMEM((4, 4, 2, 16, width), BF16),
            pltpu.VMEM((4, 4, 2, 16, width), BF16),
            pltpu.VMEM((4, 4, 2, 2, 16, width), BF16),
            pltpu.VMEM((slots, width), F32),
            pltpu.VMEM((8, count), F32),
            pltpu.VMEM((16, 128), BF16),
            pltpu.VMEM((4, 4, 2, 16, 128), BF16),
            pltpu.VMEM((depth, half), BF16),
            pltpu.VMEM((depth, half), BF16),
            pltpu.VMEM((depth, half), BF16),
            pltpu.VMEM((8, 48, half), BF16),
            pltpu.VMEM((48, half), BF16),
            pltpu.VMEM((8, 48, 128), BF16),
            pltpu.VMEM((2, 24, 128), F32),
            pltpu.VMEM((24, width), F32),
            dma, dma, dma, dma, dma, dma, dma, dma, dma((2,)), dma((2,)), dma((4, 2)), dma((4, 2)),
            dma, dma, dma((2,)), dma((2,)), dma((4, 2)), dma((4, 2)),
            dma((4,)), dma((4,)), dma((4,)), dma((4,)), dma, dma,
            dma((2,)), dma((2,)), dma((2,)), dma((2,)), dma((2,)), dma((2,)),
            dma((2,)), dma((2,)), dma((2,)), dma((2,)), dma((2,)), dma((2,)), dma((2,)), dma((2,)),
            dma((4,)), dma((4,)), dma((4,)), dma((4,)), dma((8,)), dma((8,)), dma((8,)), dma((8,)),
            dma((8,)), dma((8,)), dma((4,)), dma((4,)), dma((5,)),
            dma, dma, dma((8,)), dma((8,)), dma((8,)), dma((8,)), dma((16,)), dma((11,)),
        ],
        compiler_params=pltpu.CompilerParams(
            collective_id=1, has_side_effects=True, vmem_limit_bytes=62 << 20
        ),
    )(
        tokens, widen_weight, narrow_weight.T, head_weight.T, predictor_rows, owner_of, token_of
    )


def body(
    tokens, widen_weight, narrow_weight, head_weight, predictor_rows, target_index, destination
):
    devices = lax.axis_size("tgt") * lax.axis_size("fsdp") * lax.axis_size("dp")
    entries = target_index.shape[0]
    return move(*step(
        tokens, widen_weight, narrow_weight, head_weight, predictor_rows,
        destination.reshape(1, entries), target_index.reshape(1, entries),
        1.0 / math.sqrt(entries * devices),
    ))


def move_kernel(a, b, d, a_out, b_out, d_out):
    a_out[...] = a[...]
    b_out[...] = b[...]
    d_out[...] = d[...]


def move(a, b, d):
    wide = a.shape[1]
    first = pl.BlockSpec((a.shape[0] // 4, wide), lambda i: (i, 0))
    second = pl.BlockSpec((b.shape[0] // 4, wide), lambda i: (i, 0))
    third = pl.BlockSpec(d.shape, lambda i: (0, 0))
    return pl.pallas_call(
        move_kernel,
        grid=(4,),
        out_shape=tuple(jax.ShapeDtypeStruct(o.shape, o.dtype) for o in (a, b, d)),
        in_specs=[first, second, third],
        out_specs=(first, second, third),
    )(a, b, d)


def solution(mesh):
    in_specs = (
        P(("tgt", "fsdp", "dp"), None),
        P(None, "fsdp"),
        P(None, "fsdp"),
        P(None, "fsdp"),
        P(("tgt", "fsdp", "dp"), None),
        P(("tgt", "fsdp", "dp")),
        P(("tgt", "fsdp", "dp"), None),
    )
    out_specs = (P(("tgt", "fsdp", "dp"), None), P(("tgt", "fsdp", "dp"), None), P("fsdp", None))
    return jax.shard_map(body, mesh=mesh, in_specs=in_specs, out_specs=out_specs, check_vma=False)
```

```python
import functools
import math

import jax
import jax.numpy as jnp
from jax import lax
from jax.experimental import pallas as pl
from jax.experimental.pallas import tpu as pltpu
from jax.sharding import PartitionSpec as P

MESH = pl.DeviceIdType.MESH
F32, BF16 = jnp.float32, jnp.bfloat16


def norm_rows(values):
    center = jnp.mean(values, axis=-1, keepdims=True)
    shifted = values - center
    spread = jnp.mean(shifted * shifted, axis=-1, keepdims=True)
    return shifted * lax.rsqrt(spread + 1e-06)


def place():
    t, f, d = lax.axis_index("tgt"), lax.axis_index("fsdp"), lax.axis_index("dp")
    return lax.rem(f // 2, 4), d, 2 * t + f // 8, lax.rem(f, 2)


def device(x, y, z, c):
    return (z // 2, lax.rem(z, 2) * 8 + x * 2 + c, y)


def send(src, dst, send_sem, recv_sem, target):
    copy = pltpu.make_async_remote_copy(src, dst, send_sem, recv_sem, device_id=target, device_id_type=MESH)
    copy.start()


def wait_recv(dst, sem, target):
    pltpu.make_async_remote_copy(dst, dst, sem, sem, device_id=target, device_id_type=MESH).wait_recv()


def wait_send(src, sem, target):
    pltpu.make_async_remote_copy(src, src, sem, sem, device_id=target, device_id_type=MESH).wait_send()


def gelu(v):
    return 0.5 * v * (1.0 + lax.erf(v * math.sqrt(0.5)))


def kernel(
    factor, cap, tokens, widen, narrow_in, head_t, rows_in, owner_of, token_of, feats_out, error_out, grad,
    narrow_t, rows, feats, error, xs, w1, w2, hid, nar, nar_in, heads, head, kept, pp_out, pp_in, pc_out, pc_in, py_out, py_in, summed,
    buf_x, buf_z, mid_x, mid_z, rcv, pred, slot_of, flags, flags_in, pair_out, pair_in, shares, r1, r_own, r2, fin, gout,
    s_xp, r_xp, s_xy, r_xy, s_xf, r_xf, s_wp, r_wp, s_wx, r_wx, s_wz, r_wz,
    s_np, r_np, s_nx, r_nx, s_nz, r_nz, s_hx, r_hx, s_hz, r_hz, s_hp, r_hp,
    s_pp, r_pp, s_pc, r_pc, s_py, r_py, s_wf, r_wf, s_nf, r_nf, s_mx, r_mx, s_mf, r_mf,
    s_x, r_x, s_z, r_z, s_xz, r_xz, s_zx, r_zx, s_f, r_f, s_fz, r_fz, s_o, s_0, r_0, s_1, r_1, s_2, r_2, s_3, r_3,
):
    x, y, z, c = place()
    zl, p = lax.rem(z, 2), lax.rem(y, 2)
    partner = device(x, y, z, 1 - c)
    y_up, y_down = lax.rem(y + 1, 4), lax.rem(y + 3, 4)
    z_up = device(x, y, lax.rem(z + 1, 4), c)
    z_down = device(x, y, lax.rem(z + 3, 4), c)
    ahead = lax.select(c == 0, y_up, y_down)
    behind = lax.select(c == 0, y_down, y_up)
    helper, helped = device(x, ahead, z, c), device(x, behind, z, c)
    steps, back = (0, 1, 3, 2), (0, 2, 1, 3)

    def at_x(step):
        return lax.rem(x + step, 4)

    def across(step):
        return device(at_x(step), y, z, c)

    ring = c == zl

    t = z // 2
    me = 8 * z + 2 * x + c
    owners = 32

    def along_x(step, core=0):
        nx = lax.rem(x + step, 4)
        return device(nx, y, z, lax.rem(c + core, 2)), nx

    def along_z(step, core=0):
        nz = lax.rem(z + step, 4)
        return device(x, y, nz, lax.rem(c + core, 2)), nz

    def copy_of(j):
        nt, nd = lax.rem(t + j // 4, 2), lax.rem(y + lax.rem(j, 4), 4)
        return device(x, nd, 2 * nt + zl, c), nt * 4 + nd

    def chip(j):
        nz, nx = lax.rem(zl + j // 4, 2), lax.rem(x + lax.rem(j, 4), 4)
        return device(nx, y, 2 * t + nz, c), 4 * nz + nx


    hops = [(step, core) for core in (0, 1) for step in (1, 3, 2, 0) if step + core]
    barrier = pltpu.get_barrier_semaphore()

    others = [partner]
    others += [along(step, core)[0] for along in (along_x, along_z) for core in (0, 1) for step in (1, 2, 3)]
    others += [chip(j)[0] for j in (5, 6, 7)] + [copy_of(j)[0] for j in (1, 2, 3, 5, 6, 7)]
    others += [device(x, lax.rem(y + dy, 4), lax.rem(z + dz, 4), 1 - c) for dz in (0, 2) for dy in (1, 2, 3)]
    for other in others:
        pl.semaphore_signal(barrier, inc=1, device_id=other, device_id_type=MESH)

    pltpu.make_async_copy(narrow_in, narrow_t, s_o.at[5]).start()
    pltpu.make_async_copy(rows_in, rows, s_o.at[6]).start()
    xs[0] = norm_rows(tokens[...].astype(F32)).astype(BF16)
    pltpu.make_async_copy(narrow_in, narrow_t, s_o.at[5]).wait()
    for core in range(2):
        for k in range(4):
            unit = (8 * core + 2 * k + p) * 384
            nar[core, :88, 384 * k : 384 * (k + 1)] = narrow_t[:, pl.ds(pl.multiple_of(unit, 384), 384)]
    nar[:, 88:, :] = jnp.zeros((2, 8, 1536), BF16)
    heads[zl, x, c, :88, :] = head_t[...]
    heads[zl, x, c, 88:, :] = jnp.zeros((8, 384), BF16)
    w2[0, 704:, :] = jnp.zeros((64, 1536), BF16)
    w2[1, :64, :] = jnp.zeros((64, 1536), BF16)
    pl.semaphore_wait(barrier, len(others))

    def spread_z(at):
        send(w1.at[at, pl.ds(0, 704)], w1.at[at, pl.ds(0, 704)], s_wz.at[at, 0], r_wz.at[at, 0], z_up)
        send(w1.at[at, pl.ds(704, 704)], w1.at[at, pl.ds(704, 704)], s_wz.at[at, 1], r_wz.at[at, 1], z_down)

    def spread_x():
        for k in (1, 2):
            send(w1.at[x], w1.at[x], s_wx.at[k - 1], r_wx.at[back[k] - 1], across(steps[k]))

    def pass_x(at, k):
        half = w1.at[at, pl.ds(0, 704)] if k == 2 else w1.at[at, pl.ds(704, 704)]
        send(half, half, s_wf.at[k - 1], r_wf.at[k - 1], across(4 - steps[k]))

    @pl.when((c == p) & (c != zl))
    def _():
        send(widen, w1.at[x], s_wp, r_wp, partner)

    send(nar.at[1 - c], nar_in, s_np, r_np, partner)
    send(xs.at[0], xs.at[2 + c], s_xy, r_xy, helper)

    @pl.when((c == p) & ring)
    def _():
        w1[x] = widen[...]
        spread_x()
        spread_z(x)

    send(xs.at[0], xs.at[1], s_xp, r_xp, partner)

    @pl.when((c != p) & ring)
    def _():
        wait_recv(w1.at[x], r_wp, partner)
        spread_x()
        spread_z(x)

    def hidden(slot, at):
        block = jnp.dot(xs[slot], w1[at], preferred_element_type=F32)
        hid[slot, :, pl.ds(pl.multiple_of(at * 384, 384), 384)] = gelu(block).astype(BF16)

    def all_hidden(at):
        def fill(slot, _):
            hidden(slot, at)
            return 0

        lax.fori_loop(0, 4, fill, 0)

    def half_hidden(first, at):
        hidden(first, at)
        hidden(first + 1, at)

    def piece(side, at):
        return pl.multiple_of(64 * side + 176 * at, 16)

    def upper(side, at):
        return w2.at[side, pl.ds(piece(side, at), 96)]

    def lower(side, at):
        return w2.at[side, pl.ds(pl.multiple_of(piece(side, at) + 96, 16), 80)]

    def part(side, at, first, count):
        return w2.at[side, pl.ds(pl.multiple_of(piece(side, at) + first, 16), count)]

    def spread_narrow_z(at, top, bottom):
        up, down = part(zl, at, 0, top), part(zl, at, 176 - bottom, bottom)
        send(up, up, s_nz.at[at, 0], r_nz.at[at, 0], z_up)
        send(down, down, s_nz.at[at, 1], r_nz.at[at, 1], z_down)

    def narrow_z(at, top, bottom):
        wait_recv(part(1 - zl, at, 0, top), r_nz.at[at, 0], partner)
        wait_recv(part(1 - zl, at, 176 - bottom, bottom), r_nz.at[at, 1], partner)

    def middle_out():
        narrow_z(x, 96, 80)
        rows_mid = part(1 - zl, x, 64, 64)
        for k in (1, 2):
            send(rows_mid, rows_mid, s_mx.at[k - 1], r_mx.at[back[k] - 1], across(steps[k]))

    def middle_pass():
        for k in (1, 2):
            at = at_x(steps[k])
            wait_recv(part(1 - zl, at, 64, 64), r_mx.at[k - 1], partner)
            half = part(1 - zl, at, 64 if k == 2 else 96, 32)
            send(half, half, s_mf.at[k - 1], r_mf.at[k - 1], across(4 - steps[k]))

    def middle_far():
        wait_recv(part(1 - zl, at_x(2), 64, 32), r_mf.at[1], partner)
        wait_recv(part(1 - zl, at_x(2), 96, 32), r_mf.at[0], partner)

    own_cols = w2.at[zl, pl.ds(piece(zl, x), 176)]
    own_head = heads.at[zl, x, c]

    def spread_narrow_x():
        for k in (1, 2):
            send(own_cols, own_cols, s_nx.at[k - 1], r_nx.at[back[k] - 1], across(steps[k]))

    def spread_head_x():
        for k in (1, 2, 3):
            send(own_head, own_head, s_hx.at[k], r_hx.at[back[k]], across(steps[k]))

    def spread_head_z(at):
        src = heads.at[zl, at, c]

        @pl.when(lax.rem(at, 2) == 0)
        def _():
            send(src, src, s_hz.at[at], r_hz.at[at], z_up)

        @pl.when(lax.rem(at, 2) == 1)
        def _():
            send(src, src, s_hz.at[at], r_hz.at[at], z_down)

    def widen_near():
        for k in (1, 2):
            at = at_x(steps[k])
            wait_recv(w1.at[at], r_wx.at[k - 1], partner)
            pass_x(at, k)
            spread_z(at)

    def widen_far():
        at = at_x(2)
        wait_recv(w1.at[at, pl.ds(0, 704)], r_wf.at[1], partner)
        wait_recv(w1.at[at, pl.ds(704, 704)], r_wf.at[0], partner)
        spread_z(at)

    def widen_z(at):
        wait_recv(w1.at[at, pl.ds(0, 704)], r_wz.at[at, 0], partner)
        wait_recv(w1.at[at, pl.ds(704, 704)], r_wz.at[at, 1], partner)

    def narrow_near():
        for k in (1, 2):
            at = at_x(steps[k])
            wait_recv(w2.at[zl, pl.ds(piece(zl, at), 176)], r_nx.at[k - 1], partner)
            half = (upper if k == 2 else lower)(zl, at)
            send(half, half, s_nf.at[k - 1], r_nf.at[k - 1], across(4 - steps[k]))
            spread_narrow_z(at, 64, 48)

    def narrow_far():
        at = at_x(2)
        wait_recv(upper(zl, at), r_nf.at[1], partner)
        wait_recv(lower(zl, at), r_nf.at[0], partner)
        spread_narrow_z(at, 64, 48)

    def indices():
        count = owner_of.shape[1]
        owner = owner_of[...]
        one = jnp.where(lax.broadcasted_iota(jnp.int32, (128, count), 0) == owner, 1.0, 0.0)
        before = lax.broadcasted_iota(jnp.int32, (count, count), 0) < lax.broadcasted_iota(
            jnp.int32, (count, count), 1
        )
        rank = jnp.dot(one.astype(BF16), jnp.where(before, 1.0, 0.0).astype(BF16), preferred_element_type=F32)
        rank = jnp.sum(rank * one, axis=0, keepdims=True)
        flags[...] = lax.dot_general(
            jnp.ones((16, count), BF16), one.astype(BF16), (((1,), (1,)), ((), ())), preferred_element_type=F32
        ).astype(BF16)
        flags_in[z, x, c] = flags[...]
        line = lax.broadcasted_iota(jnp.int32, (8, count), 0)
        known = jnp.where(line == 0, owner.astype(F32) + 1.0, rank).astype(BF16)
        here = lax.broadcasted_iota(jnp.int32, (tokens.shape[0], count), 0) == token_of[...]
        found = lax.dot_general(
            known, jnp.where(here, 1.0, 0.0).astype(BF16), (((1,), (1,)), ((), ())), preferred_element_type=F32
        )
        slot_of[...] = jnp.broadcast_to((found[0:1] - 1.0) * cap + found[1:2], slot_of.shape)

        for step, core in hops:
            at = 2 * step + core
            send(flags, flags_in.at[z, x, c], s_f.at[at], r_f.at[at], along_x(step, core)[0])

    def spread_flags():
        for step, core in hops:
            source = flags_in.at[z, lax.rem(x + 4 - step, 4), lax.rem(c + core, 2)]
            wait_recv(source, r_f.at[2 * step + core], partner)
        for step in (1, 3, 2):
            send(flags_in.at[z], flags_in.at[z], s_fz.at[step], r_fz.at[step], along_z(step)[0])

    def neighbour_rows(at):
        wait_recv(xs.at[2 + c], r_xy, partner)
        send(xs.at[2 + c], xs.at[2 + c], s_xf, r_xf, partner)
        hidden(2 + c, at)
        wait_recv(xs.at[3 - c], r_xf, partner)
        hidden(3 - c, at)

    wait_recv(nar_in, r_np, partner)
    mine, other = nar[c, :88, :].astype(F32), nar_in[:88, :].astype(F32)

    @pl.when(c == 0)
    def _():
        own_cols[...] = jnp.concatenate([mine, other], axis=0).astype(BF16)

    @pl.when(c == 1)
    def _():
        own_cols[...] = jnp.concatenate([other, mine], axis=0).astype(BF16)

    spread_narrow_z(x, 96, 80)

    @pl.when(ring)
    def _():
        hidden(0, x)
        wait_recv(xs.at[1], r_xp, partner)
        hidden(1, x)
        widen_near()
        spread_narrow_x()
        middle_out()
        indices()
        neighbour_rows(x)
        half_hidden(0, at_x(1))
        widen_far()
        half_hidden(2, at_x(1))
        narrow_near()
        half_hidden(0, at_x(3))
        middle_pass()
        half_hidden(2, at_x(3))
        narrow_far()
        all_hidden(at_x(2))

    @pl.when(jnp.logical_not(ring))
    def _():
        spread_narrow_x()
        widen_z(x)
        hidden(0, x)
        wait_recv(xs.at[1], r_xp, partner)
        hidden(1, x)
        narrow_near()
        middle_out()
        indices()
        neighbour_rows(x)
        narrow_far()
        middle_pass()
        for k in (1, 2, 3):
            widen_z(at_x(steps[k]))
            all_hidden(at_x(steps[k]))

    spread_head_x()
    spread_head_z(x)
    spread_flags()

    def partial(slot, side):
        return lax.dot_general(
            hid[slot], w2[side], (((1,), (1,)), ((), ())), preferred_element_type=F32
        )

    def add(value, side):
        @pl.when(side == 0)
        def _():
            summed[:, :768] += value

        @pl.when(side == 1)
        def _():
            summed[:, 640:] += value

    summed[...] = tokens[...].astype(F32)
    for turn in range(2):
        side = zl if turn == 0 else 1 - zl
        if turn == 1:
            middle_far()
            for k in (1, 2, 3):
                narrow_z(at_x(steps[k]), 64, 48)
        pc_out[turn] = partial(3 - c, side).astype(BF16)
        send(pc_out.at[turn], pc_in.at[turn], s_pc.at[turn], r_pc.at[turn], partner)
        kept[...] = partial(2 + c, side)
        wait_recv(pc_in.at[turn], r_pc.at[turn], partner)
        py_out[turn] = (kept[...] + pc_in[turn].astype(F32)).astype(BF16)
        send(py_out.at[turn], py_in.at[turn], s_py.at[turn], r_py.at[turn], helped)
        pp_out[turn] = partial(1, side).astype(BF16)
        send(pp_out.at[turn], pp_in.at[turn], s_pp.at[turn], r_pp.at[turn], partner)
        add(partial(0, side), side)
        if turn == 0:
            for k in (1, 2, 3):
                at = at_x(steps[k])
                wait_recv(heads.at[zl, at, c], r_hx.at[k], partner)
                spread_head_z(at)

    for k in range(4):
        at = at_x(steps[k])
        wait_recv(heads.at[1 - zl, at, c], r_hz.at[at], partner)
    send(heads.at[:, :, c], heads.at[:, :, c], s_hp, r_hp, partner)
    for turn in range(2):
        side = zl if turn == 0 else 1 - zl
        wait_recv(pp_in.at[turn], r_pp.at[turn], partner)
        add(pp_in[turn].astype(F32), side)
        wait_recv(py_in.at[turn], r_py.at[turn], partner)
        add(py_in[turn].astype(F32), side)
    feats[...] = norm_rows(summed[...]).astype(BF16)
    pltpu.make_async_copy(feats, feats_out, s_o.at[4]).start()


    line = lax.broadcasted_iota(jnp.int32, (128, feats.shape[0]), 0)
    outer, inner = line // 32, lax.rem(line // 16, 2) * cap + lax.rem(line, 16)

    def rows_for(slot):
        pick = jnp.where(slot.astype(F32) == slot_of[0:1], 1.0, 0.0).astype(BF16)
        return jnp.dot(pick, feats[...], preferred_element_type=F32).astype(BF16).reshape(4, 2, 16, -1)

    for step in (1, 3, 2):
        target, nx = along_x(step)
        buf_x[nx] = rows_for(outer * (8 * cap) + inner + nx * (2 * cap))
        send(buf_x.at[nx], mid_x.at[x], s_x.at[step], r_x.at[step], target)
        target, nz = along_z(step)
        buf_z[nz] = rows_for(outer * (2 * cap) + inner + nz * (8 * cap) + 16)
        send(buf_z.at[nz], mid_z.at[z], s_z.at[step], r_z.at[step], target)
    mid_x[x] = rows_for(outer * (8 * cap) + inner + x * (2 * cap))
    mid_z[z] = rows_for(outer * (2 * cap) + inner + z * (8 * cap) + 16)

    wait_recv(heads.at[:, :, 1 - c], r_hp, partner)
    for k in range(8):
        both = [heads[k // 4, k % 4, core, :88, :].astype(F32) for core in range(2)]
        head[k] = jnp.concatenate(both, axis=0).astype(BF16)

    pltpu.make_async_copy(rows_in, rows, s_o.at[6]).wait()

    def predict(i, _):
        rows_at = pl.ds(pl.multiple_of(i * 128, 128), 128)
        pred[rows_at, :] = lax.dot_general(
            rows[rows_at, :], head[...].reshape(-1, rows.shape[1]), (((1,), (1,)), ((), ())), preferred_element_type=F32
        )
        return 0

    lax.fori_loop(0, owners * cap // 128, predict, 0)
    width, half = feats.shape[1], pair_in.shape[1]
    error[:, width:] = jnp.zeros((error.shape[0], 2 * half - width), BF16)

    for step in (1, 3, 2):
        wait_recv(mid_x.at[lax.rem(x + 4 - step, 4)], r_x.at[step], partner)
        wait_recv(mid_z.at[lax.rem(z + 4 - step, 4)], r_z.at[step], partner)
    for step, core in hops:
        nc = lax.rem(c + core, 2)
        at = 2 * step + core
        target, nz = along_z(step, core)
        send(mid_x.at[:, nz, nc], rcv.at[z, :, c, 0], s_xz.at[at], r_xz.at[at], target)
        target, nx = along_x(step, core)
        send(mid_z.at[:, nx, nc], rcv.at[:, x, c, 1], s_zx.at[at], r_zx.at[at], target)
    rcv[z, :, c, 0] = mid_x[:, z, c]
    rcv[:, x, c, 1] = mid_z[:, x, c]

    for step in (1, 3, 2):
        wait_recv(flags_in.at[lax.rem(z + 4 - step, 4)], r_fz.at[step], partner)
    for step, core in hops:
        nc = lax.rem(c + core, 2)
        at = 2 * step + core
        wait_recv(rcv.at[lax.rem(z + 4 - step, 4), :, nc, 0], r_xz.at[at], partner)
        wait_recv(rcv.at[:, lax.rem(x + 4 - step, 4), nc, 1], r_zx.at[at], partner)

    per = 8

    def arrive(i, _):
        rows_at = pl.ds(pl.multiple_of(i * (per * cap), per * cap), per * cap)
        lane = lax.broadcasted_iota(jnp.int32, (per, 16, 128), 2)
        live = flags_in[i].reshape(per, 16, 128).astype(F32)
        live = jnp.sum(jnp.where(lane == me, live, 0.0), axis=2, keepdims=True)
        live = jnp.broadcast_to(live[:, None], (per, 2, 16, 1)).reshape(per * cap, 1)
        slot = lax.rem(lax.broadcasted_iota(jnp.int32, (per * cap, 1), 0), cap).astype(F32)
        got = rcv[i].astype(F32).reshape(per * cap, -1)
        wrong = jnp.where(slot < live, pred[rows_at, :] - got, 0.0).astype(BF16)
        error[rows_at, :width] = wrong
        pltpu.make_async_copy(error.at[rows_at, pl.ds(0, width)], error_out.at[rows_at], s_o.at[i]).start()
        return 0

    lax.fori_loop(0, 4, arrive, 0)

    def product(core):
        columns = error[:, pl.ds(pl.multiple_of(core * half, half), half)]
        return lax.dot_general(
            rows[...], columns, (((0,), (0,)), ((), ())), preferred_element_type=F32
        )

    pair_out[...] = product(1 - c).astype(BF16)
    send(pair_out, pair_in, s_0, r_0, partner)
    kept[...] = product(c)
    wait_recv(pair_in, r_0, partner)
    shares[...] = (kept[...] + pair_in[...].astype(F32)).astype(BF16)

    block = 48

    def share(j, _):
        target, b = chip(j)
        send(shares.at[pl.ds(pl.multiple_of(b * block, 16), block)], r1.at[j], s_1.at[j], r_1.at[j], target)
        return 0

    lax.fori_loop(1, 8, share, 0)
    own = shares[pl.ds(pl.multiple_of((4 * zl + x) * block, 16), block), :].astype(F32)

    def take(j, total):
        wait_recv(r1.at[j], r_1.at[j], partner)
        return total + r1[j].astype(F32)

    own = lax.fori_loop(1, 8, take, own)
    mine_at = t * 4 + y
    r_own[...] = own.astype(BF16)

    def holder(r, core):
        return device(x, lax.rem(r, 4), 2 * (r // 4) + zl, core)

    def columns_of(r):
        return pl.ds(pl.multiple_of(r * 128, 128), 128)

    def scatter(r, _):
        @pl.when(r != mine_at)
        def _():
            send(r_own.at[:, columns_of(r)], r2.at[mine_at], s_2.at[r], r_2.at[mine_at], holder(r, c))

        return 0

    lax.fori_loop(0, 6 - c, scatter, 0)
    made = 6 * c + mine_at

    @pl.when(mine_at < 6 - c)
    def _():
        r2[mine_at] = r_own[:, columns_of(mine_at)]

        def settle(r, _):
            @pl.when(r != mine_at)
            def _():
                wait_recv(r2.at[r], r_2.at[r], partner)

            return 0

        lax.fori_loop(0, 8, settle, 0)
        total = r2[0].astype(F32)
        for r in range(1, 8):
            total = total + r2[r].astype(F32)
        fin[...] = (total * factor).reshape(2, 24, 128)

        def hand_out(q, _):
            r, core = q // 2, lax.rem(q, 2)

            @pl.when((r != mine_at) | (core != c))
            def _():
                send(fin.at[core], gout.at[:, columns_of(made)], s_3.at[q], r_3.at[made], holder(r, core))

            return 0

        lax.fori_loop(0, 16, hand_out, 0)
        gout[:, columns_of(made)] = fin[c]

    def collect(i, _):
        @pl.when((i != made) | (mine_at >= 6 - c))
        def _():
            wait_recv(gout.at[:, columns_of(i)], r_3.at[i], partner)

        return 0

    lax.fori_loop(0, 11, collect, 0)
    grad[...] = gout[...]

    for step in (1, 2, 3):
        wait_send(flags_in.at[z], s_fz.at[step], partner)
        wait_send(mid_x.at[x], s_x.at[step], partner)
        wait_send(mid_z.at[z], s_z.at[step], partner)
    for step, core in hops:
        at = 2 * step + core
        wait_send(flags, s_f.at[at], partner)
        wait_send(rcv.at[z, :, c, 0], s_xz.at[at], partner)
        wait_send(rcv.at[:, x, c, 1], s_zx.at[at], partner)
    pltpu.make_async_copy(feats, feats_out, s_o.at[4]).wait()
    for i in range(4):
        rows_at = pl.ds(i * per * cap, per * cap)
        pltpu.make_async_copy(error.at[rows_at, pl.ds(0, width)], error_out.at[rows_at], s_o.at[i]).wait()

    def done_shares(j, _):
        target, b = chip(j)
        wait_send(shares.at[pl.ds(pl.multiple_of(b * block, 16), block)], s_1.at[j], partner)
        return 0

    lax.fori_loop(1, 8, done_shares, 0)

    def done_scatter(r, _):
        @pl.when(r != mine_at)
        def _():
            wait_send(r_own.at[:, columns_of(r)], s_2.at[r], partner)

        return 0

    lax.fori_loop(0, 6 - c, done_scatter, 0)

    @pl.when(mine_at < 6 - c)
    def _():
        def handed(q, _):
            @pl.when((q // 2 != mine_at) | (lax.rem(q, 2) != c))
            def _():
                wait_send(fin.at[0], s_3.at[q], partner)

            return 0

        lax.fori_loop(0, 16, handed, 0)

    wait_send(pair_out, s_0, partner)
    @pl.when((c == p) & (c != zl))
    def _():
        wait_send(widen, s_wp, partner)

    wait_send(xs.at[0], s_xy, partner)
    wait_send(xs.at[0], s_xp, partner)
    wait_send(xs.at[2 + c], s_xf, partner)
    wait_send(nar.at[1 - c], s_np, partner)
    wait_send(heads.at[:, :, c], s_hp, partner)
    for k in range(4):
        at = at_x(steps[k])

        @pl.when(ring)
        def _():
            if k in (1, 2):
                wait_send(w1.at[x], s_wx.at[k - 1], partner)
                wait_send(w1.at[x, pl.ds(0, 704)], s_wf.at[k - 1], partner)
            wait_send(w1.at[at, pl.ds(0, 704)], s_wz.at[at, 0], partner)
            wait_send(w1.at[at, pl.ds(704, 704)], s_wz.at[at, 1], partner)

        if k in (1, 2):
            wait_send(own_cols, s_nx.at[k - 1], partner)
            wait_send((upper if k == 2 else lower)(zl, x), s_nf.at[k - 1], partner)
            wait_send(part(zl, x, 0, 64), s_mx.at[k - 1], partner)
            wait_send(part(zl, x, 0, 32), s_mf.at[k - 1], partner)
        if k:
            wait_send(own_head, s_hx.at[k], partner)
        wait_send(part(zl, at, 0, 64 if k else 96), s_nz.at[at, 0], partner)
        wait_send(part(zl, at, 0, 48 if k else 80), s_nz.at[at, 1], partner)
        wait_send(heads.at[zl, at, c], s_hz.at[at], partner)
    for turn in range(2):
        wait_send(pc_out.at[turn], s_pc.at[turn], partner)
        wait_send(py_out.at[turn], s_py.at[turn], partner)
        wait_send(pp_out.at[turn], s_pp.at[turn], partner)


def step(tokens, widen_weight, narrow_weight, head_weight, predictor_rows, owner_of, token_of, factor):
    count, width = tokens.shape
    slots, depth = predictor_rows.shape
    owners = lax.axis_size("tgt") * lax.axis_size("fsdp")
    cap, half = slots // owners, 768
    dma = pltpu.SemaphoreType.DMA
    vmem, hbm = pl.BlockSpec(memory_space=pltpu.VMEM), pl.BlockSpec(memory_space=pl.ANY)
    part = pltpu.VMEM((2, count, half), BF16)
    return pl.pallas_call(
        functools.partial(kernel, factor, cap),
        out_shape=(
            jax.ShapeDtypeStruct((count, width), BF16),
            jax.ShapeDtypeStruct((slots, width), BF16),
            jax.ShapeDtypeStruct((depth // lax.axis_size("fsdp"), width), F32),
        ),
        in_specs=[vmem, vmem, hbm, vmem, hbm, vmem, vmem],
        out_specs=(pl.BlockSpec(memory_space=pl.ANY), pl.BlockSpec(memory_space=pl.ANY), vmem),
        scratch_shapes=[
            pltpu.VMEM((88, narrow_weight.shape[0]), BF16),
            pltpu.VMEM((slots, depth), BF16),
            pltpu.VMEM((count, width), BF16),
            pltpu.VMEM((slots, 2 * half), BF16),
            pltpu.VMEM((4, count, width), BF16),
            pltpu.VMEM((4, width, 384), BF16),
            pltpu.VMEM((2, 768, 1536), BF16),
            pltpu.VMEM((4, count, 1536), BF16),
            pltpu.VMEM((2, 96, 1536), BF16),
            pltpu.VMEM((96, 1536), BF16),
            pltpu.VMEM((2, 4, 2, 96, depth), BF16),
            pltpu.VMEM((8, 176, depth), BF16),
            pltpu.VMEM((count, half), F32),
            part, part, part, part, part, part,
            pltpu.VMEM((count, width), F32),
            pltpu.VMEM((4, 4, 2, 16, width), BF16),
            pltpu.VMEM((4, 4, 2, 16, width), BF16),
            pltpu.VMEM((4, 4, 2, 16, width), BF16),
            pltpu.VMEM((4, 4, 2, 16, width), BF16),
            pltpu.VMEM((4, 4, 2, 2, 16, width), BF16),
            pltpu.VMEM((slots, width), F32),
            pltpu.VMEM((8, count), F32),
            pltpu.VMEM((16, 128), BF16),
            pltpu.VMEM((4, 4, 2, 16, 128), BF16),
            pltpu.VMEM((depth, half), BF16),
            pltpu.VMEM((depth, half), BF16),
            pltpu.VMEM((depth, half), BF16),
            pltpu.VMEM((8, 48, half), BF16),
            pltpu.VMEM((48, half), BF16),
            pltpu.VMEM((8, 48, 128), BF16),
            pltpu.VMEM((2, 24, 128), F32),
            pltpu.VMEM((24, width), F32),
            dma, dma, dma, dma, dma, dma, dma, dma, dma((2,)), dma((2,)), dma((4, 2)), dma((4, 2)),
            dma, dma, dma((2,)), dma((2,)), dma((4, 2)), dma((4, 2)),
            dma((4,)), dma((4,)), dma((4,)), dma((4,)), dma, dma,
            dma((2,)), dma((2,)), dma((2,)), dma((2,)), dma((2,)), dma((2,)),
            dma((2,)), dma((2,)), dma((2,)), dma((2,)), dma((2,)), dma((2,)), dma((2,)), dma((2,)),
            dma((4,)), dma((4,)), dma((4,)), dma((4,)), dma((8,)), dma((8,)), dma((8,)), dma((8,)),
            dma((8,)), dma((8,)), dma((4,)), dma((4,)), dma((7,)),
            dma, dma, dma((8,)), dma((8,)), dma((8,)), dma((8,)), dma((16,)), dma((11,)),
        ],
        compiler_params=pltpu.CompilerParams(
            collective_id=1, has_side_effects=True, vmem_limit_bytes=62 << 20
        ),
    )(
        tokens, widen_weight, narrow_weight.T, head_weight.T, predictor_rows, owner_of, token_of
    )


def body(
    tokens, widen_weight, narrow_weight, head_weight, predictor_rows, target_index, destination
):
    devices = lax.axis_size("tgt") * lax.axis_size("fsdp") * lax.axis_size("dp")
    entries = target_index.shape[0]
    return move(*step(
        tokens, widen_weight, narrow_weight, head_weight, predictor_rows,
        destination.reshape(1, entries), target_index.reshape(1, entries),
        1.0 / math.sqrt(entries * devices),
    ))


def move_kernel(a, b, d, a_out, b_out, d_out):
    a_out[...] = a[...]
    b_out[...] = b[...]
    d_out[...] = d[...]


def move(a, b, d):
    wide = a.shape[1]
    first = pl.BlockSpec((a.shape[0] // 2, wide), lambda i: (i, 0))
    second = pl.BlockSpec((b.shape[0] // 2, wide), lambda i: (i, 0))
    third = pl.BlockSpec(d.shape, lambda i: (0, 0))
    return pl.pallas_call(
        move_kernel,
        grid=(2,),
        out_shape=tuple(jax.ShapeDtypeStruct(o.shape, o.dtype) for o in (a, b, d)),
        in_specs=[first, second, third],
        out_specs=(first, second, third),
        compiler_params=pltpu.CompilerParams(vmem_limit_bytes=32 << 20),
    )(a, b, d)


def solution(mesh):
    in_specs = (
        P(("tgt", "fsdp", "dp"), None),
        P(None, "fsdp"),
        P(None, "fsdp"),
        P(None, "fsdp"),
        P(("tgt", "fsdp", "dp"), None),
        P(("tgt", "fsdp", "dp")),
        P(("tgt", "fsdp", "dp"), None),
    )
    out_specs = (P(("tgt", "fsdp", "dp"), None), P(("tgt", "fsdp", "dp"), None), P("fsdp", None))
    return jax.shard_map(body, mesh=mesh, in_specs=in_specs, out_specs=out_specs, check_vma=False)
```
